512 devices in a mesh: head: 8 (over z_hi, core), inner: 16 (over x, y), outer: 4 (over z_lo).
Axes of the slice: x: 4, y: 4, z: 16 (z_hi: 4, z_lo: 4; z = z_hi * 4 + z_lo), core: 2. Of those that a mesh axis runs over, the one named last changes fastest.
Arguments:
- queries: bfloat16 [8192, 8192], P(('inner', 'outer', 'head')), may hold values from -6 to 6
- key_head_rows: bfloat16 [8192, 1024], P(('inner', 'outer', 'head')), may hold values from -6 to 6
- value_head_rows: bfloat16 [8192, 1024], P(('inner', 'outer', 'head')), may hold values from -0.59765625 to 0.59765625
- output_gradient: bfloat16 [8192, 8192], P(('inner', 'outer', 'head')), may hold values from -6 to 6
- support_values: bfloat16 [8192, 8192], P(('inner', 'outer', 'head')), may hold values from -6 to 6
- thresholds: bfloat16 [8192, 64], P(('inner', 'outer', 'head')), may hold values from 0.3984375 to 1.1953125
- gate_row_sums: bfloat16 [8192, 64], P(('inner', 'outer', 'head')), may hold values from 10 to 100
- token_pos: int32 [8192], replicated, may hold values from 0 to 8191, as said below
- block_mask: int32 [64, 64], replicated, may hold values from 0 to 1, as said below
Outputs:
- grad_queries: bfloat16 [8192, 8192], P(('inner', 'outer', 'head'))
- key_gradient: bfloat16 [8192, 1024], P(('inner', 'outer', 'head'))
- value_gradient: bfloat16 [8192, 1024], P(('inner', 'outer', 'head'))
The draws below stay inside these ranges and needn't reach their ends.
Inputs may be any that keep to these rules, and one draw needn't show every extreme that they name: `token_pos`: A permutation of the 8192 positions in which each aligned run of 128 stored rows holds 128 consecutive positions in increasing order, the first a multiple of 128. `block_mask`: entry [a, b] is 1 where queries of position block a may see keys of position block b; the diagonal is 1.
All inputs are finite; a program needn't handle non-finite values.
Results may differ from the reference program's by a relative error of at most 0.005.
Values may be sent and summed in bfloat16 or wider, within the bound.
No kernel may reach another device: no remote copies, remote signals or barrier semaphores. Data moves between devices by JAX's collectives and lax.ppermute only.
A program may use at most 64 MiB of HBM per device.

```python
import math
import jax
import jax.numpy as jnp
from jax import lax

QUERY_HEADS = 64
KEY_HEADS = 8
HEAD_WIDTH = 128
BLK = 128
SEQUENCE_TOKENS = 8192
NB = 64


def draw_token_pos(key, part):
    key = jax.random.fold_in(key, 11)
    order = jax.random.permutation(key, jnp.arange(NB, dtype=jnp.int32))
    stored = jnp.arange(NB * BLK, dtype=jnp.int32)
    return (order[stored // BLK] * BLK + stored % BLK).astype(jnp.int32)


def draw_block_mask(key, part):
    key = jax.random.fold_in(key, 23)
    levels = jax.random.randint(key, (NB, NB), 0, 8)
    kept = (levels > 0).astype(jnp.int32)
    diagonal = jnp.arange(NB)[:, None] == jnp.arange(NB)[None, :]
    return jnp.where(diagonal, 1, kept).astype(jnp.int32)


def block_levels(key, dims, split, least, top_value):
    def one(dim, shards_of):
        draws = jax.random.uniform(jax.random.fold_in(jax.random.fold_in(key, 6), dim), (shards_of,), jnp.float32, least / len(split), top_value / len(split))
        return jnp.repeat(jnp.exp(draws), dims[dim] // shards_of).reshape((-1,) + (1,) * (len(dims) - dim - 1))

    gain = one(*split[0])
    for cut in split[1:]:
        gain = gain * one(*cut)
    return gain


def noise(own_key, extent, spread, most, shards=(), kind=jnp.bfloat16):
    level = block_levels(own_key, extent, shards, -0.22, 0.18) if shards else 1.0
    array = jax.random.normal(own_key, extent, jnp.float32) * spread * level
    return jnp.minimum(jnp.maximum(array, -most), most).astype(kind)


def setup_inputs(seed: int = 0) -> dict:
    seeds = jax.random.split(jax.random.key(seed), 10)
    return {
        "queries": noise(seeds[0], (SEQUENCE_TOKENS, QUERY_HEADS * HEAD_WIDTH), 1.0, 6.0, ((0, 512),)),
        "key_head_rows": noise(seeds[1], (SEQUENCE_TOKENS, KEY_HEADS * HEAD_WIDTH), 1.0, 6.0, ((0, 512),)),
        "value_head_rows": noise(seeds[2], (SEQUENCE_TOKENS, KEY_HEADS * HEAD_WIDTH), 0.1, 0.59765625, ((0, 512),)),
        "output_gradient": noise(seeds[3], (SEQUENCE_TOKENS, QUERY_HEADS * HEAD_WIDTH), 1.0, 6.0, ((0, 512),)),
        "support_values": noise(seeds[4], (SEQUENCE_TOKENS, QUERY_HEADS * HEAD_WIDTH), 1.0, 6.0, ((0, 512),)),
        "thresholds": jnp.clip(0.3984375 + 0.796875 * jax.random.uniform(seeds[5], (SEQUENCE_TOKENS, QUERY_HEADS), jnp.float32) ** block_levels(seeds[5], (SEQUENCE_TOKENS, QUERY_HEADS), ((0, 512),), -0.2, 0.2), 0.3984375, 1.1953125).astype(jnp.bfloat16),
        "gate_row_sums": jnp.clip(jnp.exp(math.log(100.0) - 2.3025851 * jax.random.uniform(seeds[6], (SEQUENCE_TOKENS, QUERY_HEADS), jnp.float32) ** block_levels(seeds[6], (SEQUENCE_TOKENS, QUERY_HEADS), ((0, 512),), -0.2, 0.2)), 10.0, 100.0).astype(jnp.bfloat16),
        "token_pos": draw_token_pos(jax.random.fold_in(seeds[9], 71), 0),
        "block_mask": draw_block_mask(jax.random.fold_in(seeds[9], 71), 0),
    }


def reference(queries, key_head_rows, value_head_rows, output_gradient, support_values, thresholds, gate_row_sums, token_pos, block_mask):
    head_groups = QUERY_HEADS // KEY_HEADS
    score_scale = HEAD_WIDTH ** -0.5
    query_whole = queries.reshape(SEQUENCE_TOKENS, KEY_HEADS, head_groups, HEAD_WIDTH).astype(jnp.float32)
    gradient_whole = output_gradient.reshape(SEQUENCE_TOKENS, KEY_HEADS, head_groups, HEAD_WIDTH).astype(jnp.float32)
    key_whole = key_head_rows.reshape(SEQUENCE_TOKENS, KEY_HEADS, HEAD_WIDTH).astype(jnp.float32)
    value_whole = value_head_rows.reshape(SEQUENCE_TOKENS, KEY_HEADS, HEAD_WIDTH).astype(jnp.float32)
    row_inner_product = jnp.einsum("thd,thd->th", output_gradient.reshape(SEQUENCE_TOKENS, QUERY_HEADS, HEAD_WIDTH).astype(jnp.float32), support_values.reshape(SEQUENCE_TOKENS, QUERY_HEADS, HEAD_WIDTH).astype(jnp.float32))
    offset_average = (row_inner_product / gate_row_sums.astype(jnp.float32)).reshape(SEQUENCE_TOKENS, KEY_HEADS, head_groups)
    entmax_cutoff = thresholds.astype(jnp.float32).reshape(SEQUENCE_TOKENS, KEY_HEADS, head_groups)
    key_block = token_pos // BLK

    def one_block(carried, block_index):
        key_gradient, value_gradient = carried
        first_row = block_index * BLK
        query_part = lax.dynamic_slice_in_dim(query_whole, first_row, BLK, 0)
        grad_part = lax.dynamic_slice_in_dim(gradient_whole, first_row, BLK, 0)
        query_pos = lax.dynamic_slice_in_dim(token_pos, first_row, BLK, 0)
        thresh_part = jnp.transpose(lax.dynamic_slice_in_dim(entmax_cutoff, first_row, BLK, 0), (1, 2, 0))[..., None]
        mean_part = jnp.transpose(lax.dynamic_slice_in_dim(offset_average, first_row, BLK, 0), (1, 2, 0))[..., None]
        mask_rows = block_mask[query_pos // BLK]
        allowed = (token_pos[None, :] <= query_pos[:, None]) & (mask_rows[:, key_block] == 1)
        scores = jnp.einsum("ikgd,jkd->kgij", query_part, key_whole) * score_scale
        gate_value = jnp.where(allowed, jnp.maximum(0.5 * scores - thresh_part, 0.0), 0.0)
        dprob = jnp.einsum("ikgd,jkd->kgij", grad_part, value_whole)
        dscore = (score_scale * gate_value * (dprob - mean_part)).astype(jnp.bfloat16).astype(jnp.float32)
        prob_low = (gate_value * gate_value).astype(jnp.bfloat16).astype(jnp.float32)
        query_gradient = jnp.einsum("kgij,jkd->ikgd", dscore, key_whole).astype(jnp.bfloat16)
        key_gradient = key_gradient + jnp.einsum("kgij,ikgd->jkd", dscore, query_part)
        value_gradient = value_gradient + jnp.einsum("kgij,ikgd->jkd", prob_low, grad_part)
        return (key_gradient, value_gradient), query_gradient

    empty_gradients = jnp.zeros((SEQUENCE_TOKENS, KEY_HEADS, HEAD_WIDTH), jnp.float32)
    (key_gradient, value_gradient), query_gradient = lax.scan(one_block, (empty_gradients, empty_gradients), jnp.arange(SEQUENCE_TOKENS // BLK, dtype=jnp.int32))
    return (query_gradient.reshape(SEQUENCE_TOKENS, QUERY_HEADS * HEAD_WIDTH), key_gradient.astype(jnp.bfloat16).reshape(SEQUENCE_TOKENS, KEY_HEADS * HEAD_WIDTH), value_gradient.astype(jnp.bfloat16).reshape(SEQUENCE_TOKENS, KEY_HEADS * HEAD_WIDTH))
```

```python
import functools

import jax
import jax.numpy as jnp
from jax import lax
from jax.experimental import pallas as pl
from jax.experimental.pallas import tpu as pltpu
from jax.sharding import Mesh, PartitionSpec as P

QUERY_HEADS = 64
KEY_HEADS = 8
HEAD_WIDTH = 128
BLK = 128
GROUP = 8
ROWS = 16
BATCH = 4
PIECE = 64
SCALE = HEAD_WIDTH ** (-0.5)
FAR = 1e30
STEPS = (0, 1, -1, 2)
TOKEN_AXES = ("x", "yh", "yl", "zlo", "zhi", "core")
PLANE = ("x", "yh", "yl")
KEY_AXES = ("x", "yl", "zhi")
VMEM = pltpu.VMEM
F32 = jnp.float32
BF16 = jnp.bfloat16


def vmem_call(kernel, out_shape, ins, **kw):
    return pl.pallas_call(
        kernel,
        out_shape=out_shape,
        in_specs=ins,
        out_specs=jax.tree.map(lambda _: pl.BlockSpec(memory_space=VMEM), out_shape),
        compiler_params=pltpu.CompilerParams(vmem_limit_bytes=48 << 20),
        **kw,
    )


WHOLE = pl.BlockSpec(memory_space=VMEM)
SCALARS = pl.BlockSpec(memory_space=pltpu.SMEM)


def pack_keys_kernel(k_ref, v_ref, out_ref):
    for head in range(KEY_HEADS):
        cols = slice(head * HEAD_WIDTH, (head + 1) * HEAD_WIDTH)
        key, value = k_ref[:, cols], v_ref[:, cols]
        for copy in range(4):
            out_ref[head * 4 + copy, 0] = key
            out_ref[head * 4 + copy, 1] = value


def pack_queries_kernel(q_ref, do_ref, sup_ref, thr_ref, sums_ref, out_ref):
    for head in range(KEY_HEADS):
        dests = [(head // 2) * 4 + yh * 2 + head % 2 for yh in range(2)]
        products = []
        for g in range(GROUP):
            n = head * GROUP + g
            cols = slice(n * HEAD_WIDTH, (n + 1) * HEAD_WIDTH)
            query, grad = q_ref[:, cols], do_ref[:, cols]
            for dest in dests:
                out_ref[dest, g] = query
                out_ref[dest, GROUP + g] = grad
            products.append(grad.astype(F32) * sup_ref[:, cols].astype(F32))
        row_dot = jnp.sum(jnp.concatenate(products, axis=0).T, axis=0, keepdims=True)
        mean = row_dot / sums_ref[head : head + 1, :]
        high = mean.astype(BF16).astype(F32)
        low = mean - high
        stats = jnp.concatenate(
            [thr_ref[head : head + 1, :], high, low, jnp.zeros((13, 128), F32)], axis=0
        ).astype(BF16)
        for dest in dests:
            out_ref[dest, 2 * GROUP] = stats


def attention_kernel(
    list_ref,
    count_ref,
    place_ref,
    qa_ref,
    qb_ref,
    kv0_ref,
    kv1_ref,
    kv2_ref,
    kv3_ref,
    dq_ref,
    g0_ref,
    g1_ref,
    g2_ref,
    g3_ref,
    k_s,
    v_s,
    bias_s,
    dk_s,
    dv_s,
    dqt_s,
):
    core, zhi = place_ref[0], place_ref[1]
    for c, ref in enumerate((kv0_ref, kv1_ref, kv2_ref, kv3_ref)):
        for b in range(8):
            k_s[c * 8 + b] = ref[b * 4 : b * 4 + 4, 0].reshape(PIECE, HEAD_WIDTH)
            v_s[c * 8 + b] = ref[b * 4 : b * 4 + 4, 1].reshape(PIECE, HEAD_WIDTH)
    dk_s[...] = jnp.zeros_like(dk_s)
    dv_s[...] = jnp.zeros_like(dv_s)
    row = lax.broadcasted_iota(jnp.int32, (PIECE, 256), 0)
    lane = lax.broadcasted_iota(jnp.int32, (PIECE, 256), 1)
    key_offset = (row >> 4) * 32 + core * 16 + (row & 15)
    query_core = jnp.where(lane < 128, core, 1 - core)
    query_offset = zhi * 32 + query_core * 16 + (lane & 15)
    bias_s[0] = jnp.zeros((PIECE, 256), F32)
    bias_s[1] = jnp.where(key_offset <= query_offset, 0.0, FAR)
    bias_s[2] = jnp.full((PIECE, 256), FAR, F32)

    def one_block(j, _):
        def rows(first):
            return jnp.concatenate(
                [ref[j, first : first + GROUP].reshape(128, HEAD_WIDTH) for ref in (qa_ref, qb_ref)],
                axis=0,
            )

        query, grad = rows(0), rows(GROUP)
        stats = jnp.concatenate(
            [ref[j, 2 * GROUP].astype(F32) for ref in (qa_ref, qb_ref)], axis=1
        )
        thresh = stats[0:1]
        mean = stats[1:2] + stats[2:3]
        query_t, grad_t = query.T, grad.T
        dqt_s[...] = jnp.zeros_like(dqt_s)

        def one_batch(step, _):
            entries = [list_ref[j * 32 + step * BATCH + u] for u in range(BATCH)]
            ids = [entry & 31 for entry in entries]
            keys = jnp.concatenate([k_s[i] for i in ids], axis=0)
            values = jnp.concatenate([v_s[i] for i in ids], axis=0)
            bias = jnp.concatenate([bias_s[entry >> 5] for entry in entries], axis=0)
            scores = jnp.dot(keys, query_t, preferred_element_type=F32)
            dprob = jnp.dot(values, grad_t, preferred_element_type=F32)
            gate = jnp.maximum(scores * (0.5 * SCALE) - thresh - bias, 0.0)
            probs = (gate * gate).astype(BF16)
            dscore = (SCALE * gate * (dprob - mean)).astype(BF16)
            dv = jnp.dot(probs, grad, preferred_element_type=F32)
            dk = jnp.dot(dscore, query, preferred_element_type=F32)
            dqt_s[...] += lax.dot_general(
                keys, dscore, (((0,), (0,)), ((), ())), preferred_element_type=F32
            )
            for u, i in enumerate(ids):
                dk_s[i] += dk[u * PIECE : (u + 1) * PIECE]
                dv_s[i] += dv[u * PIECE : (u + 1) * PIECE]
            return 0

        lax.fori_loop(0, (count_ref[j] + BATCH - 1) // BATCH, one_batch, 0)
        dq = dqt_s[...].T.astype(BF16)
        dq_ref[j, core] = dq[:128]
        dq_ref[j, 1 - core] = dq[128:]
        return 0

    lax.fori_loop(0, 16, one_block, 0)
    for c, ref in enumerate((g0_ref, g1_ref, g2_ref, g3_ref)):
        for b in range(8):
            ref[b * 4 : b * 4 + 4, 0] = dk_s[c * 8 + b].astype(BF16).reshape(4, ROWS, HEAD_WIDTH)
            ref[b * 4 : b * 4 + 4, 1] = dv_s[c * 8 + b].astype(BF16).reshape(4, ROWS, HEAD_WIDTH)


def sum_queries_kernel(in_ref, out_ref):
    for head in range(KEY_HEADS):
        parts = [
            in_ref[(((head // 2) * 2 + yh) * 2 + head % 2) * 2 + core].astype(F32)
            for yh in range(2)
            for core in range(2)
        ]
        total = ((parts[0] + parts[1]) + (parts[2] + parts[3])).astype(BF16)
        for g in range(GROUP):
            n = head * GROUP + g
            out_ref[:, n * HEAD_WIDTH : (n + 1) * HEAD_WIDTH] = total[g * ROWS : (g + 1) * ROWS]


def sum_keys_kernel(in_ref, dk_ref, dv_ref):
    for head in range(KEY_HEADS):
        cols = slice(head * HEAD_WIDTH, (head + 1) * HEAD_WIDTH)
        for kind, ref in enumerate((dk_ref, dv_ref)):
            parts = [in_ref[head * 4 + zhi, kind].astype(F32) for zhi in range(4)]
            ref[:, cols] = ((parts[0] + parts[1]) + (parts[2] + parts[3])).astype(BF16)


def exchange(value, axes):
    return lax.all_to_all(value, axes, split_axis=0, concat_axis=0, tiled=True)


def along_z(value, steps):
    pairs = [(z, (z + steps) % 16) for z in range(16)]
    return lax.ppermute(value, ("zhi", "zlo"), pairs)


def active_lists(token_pos, block_mask):
    yh, zlo = lax.axis_index("yh"), lax.axis_index("zlo")
    block_ids = token_pos.reshape(64, BLK)[:, 0] // BLK
    by_place = block_ids.reshape(16, 4)
    query_pos = lax.dynamic_index_in_dim(by_place, zlo, 1, keepdims=False)
    mine = lax.dynamic_index_in_dim(block_ids.reshape(4, 2, 2, 4), yh, 1, keepdims=False)
    key_pos = jnp.concatenate(
        [
            lax.dynamic_index_in_dim(mine, (zlo + step) % 4, 2, keepdims=False).reshape(8)
            for step in STEPS
        ]
    )
    span = jnp.arange(64, dtype=jnp.int32)
    pick_query = (query_pos[:, None] == span[None, :]).astype(BF16)
    pick_key = (key_pos[:, None] == span[None, :]).astype(BF16)
    seen = jnp.dot(
        jnp.dot(pick_query, (block_mask == 1).astype(BF16), preferred_element_type=F32).astype(BF16),
        pick_key.T,
        preferred_element_type=F32,
    )
    active = (seen > 0.5) & (key_pos[None, :] <= query_pos[:, None])
    same = key_pos[None, :] == query_pos[:, None]
    number = jnp.arange(32, dtype=jnp.int32)
    ones = active.astype(jnp.int32)
    before = jnp.sum(
        jnp.where(number[None, None, :] < number[None, :, None], ones[:, None, :], 0), axis=2
    )
    count = jnp.sum(ones, axis=1)
    code = number[None, :] + 32 * same.astype(jnp.int32)
    lists = jnp.sum(
        jnp.where(active[:, None, :] & (before[:, None, :] == number[None, :, None]), code[:, None, :], 0),
        axis=2,
    )
    lists = jnp.where(number[None, :] < count[:, None], lists, 64)
    return lists.reshape(512), count


def local(
    queries,
    key_head_rows,
    value_head_rows,
    output_gradient,
    support_values,
    thresholds,
    gate_row_sums,
    token_pos,
    block_mask,
):
    shape = jax.ShapeDtypeStruct
    send_keys = vmem_call(
        pack_keys_kernel, shape((32, 2, ROWS, HEAD_WIDTH), BF16), [WHOLE] * 2
    )(key_head_rows, value_head_rows)
    keys_own = exchange(send_keys, KEY_AXES)
    keys_near = [along_z(keys_own, -step) for step in STEPS[1:]]

    def by_head(stat):
        return stat.astype(F32).T.reshape(KEY_HEADS, GROUP * ROWS)

    send_queries = vmem_call(
        pack_queries_kernel, shape((16, 2 * GROUP + 1, ROWS, HEAD_WIDTH), BF16), [WHOLE] * 5
    )(queries, output_gradient, support_values, by_head(thresholds), by_head(gate_row_sums))
    send_queries, keys_own = lax.optimization_barrier((send_queries, keys_own))
    queries_own = exchange(send_queries, PLANE)
    queries_other = lax.ppermute(queries_own, "core", [(0, 1), (1, 0)])

    lists, count = active_lists(token_pos, block_mask)
    place = jnp.stack([lax.axis_index("core"), lax.axis_index("zhi")]).astype(jnp.int32)

    piece_shape = shape((32, 2, ROWS, HEAD_WIDTH), BF16)
    grad_query, *grad_keys = vmem_call(
        attention_kernel,
        [shape((16, 2, 128, HEAD_WIDTH), BF16)] + [piece_shape] * 4,
        [SCALARS] * 3 + [WHOLE] * 6,
        scratch_shapes=[
            VMEM((32, PIECE, HEAD_WIDTH), BF16),
            VMEM((32, PIECE, HEAD_WIDTH), BF16),
            VMEM((3, PIECE, 256), F32),
            VMEM((32, PIECE, HEAD_WIDTH), F32),
            VMEM((32, PIECE, HEAD_WIDTH), F32),
            VMEM((HEAD_WIDTH, 256), F32),
        ],
        cost_estimate=pl.CostEstimate(
            flops=10 * 256 * PIECE * HEAD_WIDTH * 256, bytes_accessed=8 << 20, transcendentals=0
        ),
    )(lists, count, place, queries_own, queries_other, keys_own, *keys_near)

    back_near = [along_z(grad, step) for grad, step in zip(grad_keys[1:], STEPS[1:])]
    back_query = exchange(grad_query.reshape(32, 128, HEAD_WIDTH), PLANE + ("core",))
    query_out = vmem_call(
        sum_queries_kernel, shape((ROWS, QUERY_HEADS * HEAD_WIDTH), BF16), [WHOLE]
    )(back_query)
    total = grad_keys[0].astype(F32)
    for part in back_near:
        total = total + part.astype(F32)
    back_keys = exchange(total.astype(BF16), KEY_AXES)
    key_shape = shape((ROWS, KEY_HEADS * HEAD_WIDTH), BF16)
    key_out, value_out = vmem_call(sum_keys_kernel, [key_shape, key_shape], [WHOLE])(back_keys)
    return query_out, key_out, value_out


def solution(mesh):
    parts = Mesh(
        mesh.devices.reshape(4, 2, 4, 2, 2, 4), ("zhi", "core", "x", "yh", "yl", "zlo")
    )
    rows = P(TOKEN_AXES, None)
    return jax.shard_map(
        local,
        mesh=parts,
        in_specs=(rows,) * 7 + (P(), P()),
        out_specs=(rows,) * 3,
        check_vma=False,
    )
```

```python
import functools

import jax
import jax.numpy as jnp
from jax import lax
from jax.experimental import pallas as pl
from jax.experimental.pallas import tpu as pltpu
from jax.sharding import Mesh, PartitionSpec as P

QUERY_HEADS = 64
KEY_HEADS = 8
HEAD_WIDTH = 128
BLK = 128
GROUP = 8
ROWS = 16
BATCH = 8
UNROLL = 3
SLOTS = 2 * GROUP + 3
PIECE = 64
SCALE = HEAD_WIDTH ** (-0.5)
FAR = 1e30
STEPS = (0, 1, -1, 2)
TOKEN_AXES = ("x", "yh", "yl", "zlo", "zhi", "core")
PLANE = ("x", "yh", "yl")
QUARTER = 4
VMEM = pltpu.VMEM
F32 = jnp.float32
BF16 = jnp.bfloat16


def vmem_call(kernel, out_shape, ins, **kw):
    return pl.pallas_call(
        kernel,
        out_shape=out_shape,
        in_specs=ins,
        out_specs=jax.tree.map(lambda _: pl.BlockSpec(memory_space=VMEM), out_shape),
        compiler_params=pltpu.CompilerParams(vmem_limit_bytes=48 << 20),
        **kw,
    )


WHOLE = pl.BlockSpec(memory_space=VMEM)
SCALARS = pl.BlockSpec(memory_space=pltpu.SMEM)


def pack_kernel(q_ref, do_ref, sup_ref, thr_ref, sums_ref, k_ref, v_ref, out_ref):
    for head in range(KEY_HEADS):
        dests = [(head // 2) * 4 + yh * 2 + head % 2 for yh in range(2)]
        products = []
        for g in range(GROUP):
            n = head * GROUP + g
            cols = slice(n * HEAD_WIDTH, (n + 1) * HEAD_WIDTH)
            query, grad = q_ref[:, cols], do_ref[:, cols]
            for dest in dests:
                out_ref[dest, g] = query
                out_ref[dest, GROUP + g] = grad
            products.append(grad.astype(F32) * sup_ref[:, cols].astype(F32))
        row_dot = jnp.sum(jnp.concatenate(products, axis=0).T, axis=0, keepdims=True)
        mean = row_dot / sums_ref[head : head + 1, :]
        high = mean.astype(BF16).astype(F32)
        low = mean - high
        stats = jnp.concatenate(
            [thr_ref[head : head + 1, :], high, low, jnp.zeros((13, 128), F32)], axis=0
        ).astype(BF16)
        cols = slice(head * HEAD_WIDTH, (head + 1) * HEAD_WIDTH)
        for dest in dests:
            out_ref[dest, 2 * GROUP] = stats
            out_ref[dest, 2 * GROUP + 1] = k_ref[:, cols]
            out_ref[dest, 2 * GROUP + 2] = v_ref[:, cols]


def attention_kernel(
    list_ref,
    count_ref,
    place_ref,
    qa_ref,
    qb_ref,
    own_ref,
    up_ref,
    down_ref,
    far_a_ref,
    far_b_ref,
    dq_ref,
    own_out,
    up_out,
    down_out,
    far_a_out,
    far_b_out,
    k_s,
    v_s,
    bias_s,
    dk_s,
    dv_s,
    dqt_s,
    q_s,
    do_s,
    stat_s,
    work_s,
):
    core, zhi = place_ref[0], place_ref[1]
    ins = [own_ref, up_ref, down_ref, far_a_ref, far_b_ref]
    outs = [own_out, up_out, down_out, far_a_out, far_b_out]
    places = [(0, 8), (8, 8), (16, 8), (24, 4), (28, 4)]
    for ref, (first, many) in zip(ins, places):
        for b in range(many):
            k_s[first + b] = ref[b, :, 0].reshape(PIECE, HEAD_WIDTH)
            v_s[first + b] = ref[b, :, 1].reshape(PIECE, HEAD_WIDTH)
    dk_s[...] = jnp.zeros_like(dk_s)
    dv_s[...] = jnp.zeros_like(dv_s)
    dqt_s[...] = jnp.zeros_like(dqt_s)
    row = lax.broadcasted_iota(jnp.int32, (PIECE, 256), 0)
    lane = lax.broadcasted_iota(jnp.int32, (PIECE, 256), 1)
    part = row >> 4
    step = jnp.where(part == 0, 0, jnp.where(part == 1, 1, jnp.where(part == 2, 3, 2)))
    key_offset = ((zhi + step) & 3) * 32 + core * 16 + (row & 15)
    query_core = jnp.where(lane < 128, core, 1 - core)
    query_offset = zhi * 32 + query_core * 16 + (lane & 15)
    bias_s[0] = jnp.zeros((PIECE, 256), F32)
    bias_s[1] = jnp.where(key_offset <= query_offset, 0.0, FAR)
    bias_s[2] = jnp.full((PIECE, 256), FAR, F32)

    def prepare(j, total):
        pair = (qa_ref, qb_ref)
        tile = (GROUP * ROWS, HEAD_WIDTH)
        q_s[j] = jnp.concatenate([ref[j, :GROUP].reshape(tile) for ref in pair], axis=0)
        do_s[j] = jnp.concatenate(
            [ref[j, GROUP : 2 * GROUP].reshape(tile) for ref in pair], axis=0
        )
        stats = jnp.concatenate([ref[j, 2 * GROUP].astype(F32) for ref in pair], axis=1)
        stat_s[j, 0:1] = stats[0:1]
        stat_s[j, 1:2] = stats[1:2] + stats[2:3]

        def put(batch, at):
            work_s[at] = j * 32 + batch * BATCH
            return at + 1

        return lax.fori_loop(0, (count_ref[j] + BATCH - 1) // BATCH, put, total)

    total = lax.fori_loop(0, 16, prepare, jnp.int32(0))
    for extra in range(UNROLL - 1):
        work_s[total + extra] = 512

    def contract(a, b, a_dim, b_dim):
        return lax.dot_general(
            a, b, (((a_dim,), (b_dim,)), ((), ())), preferred_element_type=F32
        )

    def one_step(step, _):
        results = []
        for way in range(UNROLL):
            base = work_s[step * UNROLL + way]
            j = jnp.minimum(base >> 5, 15)
            entries = [list_ref[base + u] for u in range(BATCH)]
            ids = [entry & 31 for entry in entries]
            keys = jnp.concatenate([k_s[i] for i in ids], axis=0)
            values = jnp.concatenate([v_s[i] for i in ids], axis=0)
            bias = jnp.concatenate([bias_s[entry >> 5] for entry in entries], axis=0)
            query, grad = q_s[j], do_s[j]
            scores = contract(keys, query, 1, 1)
            dprob = contract(values, grad, 1, 1)
            gate = jnp.maximum(scores * (0.5 * SCALE) - stat_s[j, 0:1] - bias, 0.0)
            probs = (gate * gate).astype(BF16)
            dscore = (SCALE * gate * (dprob - stat_s[j, 1:2])).astype(BF16)
            dv = contract(probs, grad, 1, 0)
            dk = contract(dscore, query, 1, 0)
            results.append((j, ids, dk, dv, contract(keys, dscore, 0, 0)))
        for j, ids, dk, dv, dqt in results:
            dqt_s[j] += dqt
            for u, i in enumerate(ids):
                dk_s[i] += dk[u * PIECE : (u + 1) * PIECE]
                dv_s[i] += dv[u * PIECE : (u + 1) * PIECE]
        return 0

    lax.fori_loop(0, (total + UNROLL - 1) // UNROLL, one_step, 0)

    def finish(j, _):
        dq = dqt_s[j].T.astype(BF16)
        dq_ref[j, core] = dq[:128]
        dq_ref[j, 1 - core] = dq[128:]
        return 0

    lax.fori_loop(0, 16, finish, 0)
    for ref, (first, many) in zip(outs, places):
        for b in range(many):
            for kind, sums in enumerate((dk_s, dv_s)):
                ref[b, :, kind] = sums[first + b].astype(BF16).reshape(4, ROWS, HEAD_WIDTH)


def total_kernel(own_ref, up_ref, down_ref, far_a_ref, far_b_ref, o0_ref, o1_ref, o2_ref, o3_ref):
    for b in range(8):
        far = far_a_ref[b] if b < 4 else far_b_ref[b - 4]
        total = (own_ref[b].astype(F32) + up_ref[b].astype(F32)) + (
            down_ref[b].astype(F32) + far.astype(F32)
        )
        for part, ref in enumerate((o0_ref, o1_ref, o2_ref, o3_ref)):
            ref[b] = total[part].astype(ref.dtype)


def merge_kernel(place_ref, dq_ref, o0_ref, o1_ref, o2_ref, o3_ref, out_ref):
    yh, core = place_ref[2], place_ref[0]
    for chip in range(16):
        for c in range(2):
            out_ref[chip * 2 + c, :GROUP] = dq_ref[chip, c].reshape(GROUP, ROWS, HEAD_WIDTH)
            out_ref[chip * 2 + c, GROUP:] = jnp.zeros((2, ROWS, HEAD_WIDTH), BF16)
    for b in range(8):
        total = (o0_ref[b] + o1_ref[b].astype(F32)) + (
            o2_ref[b].astype(F32) + o3_ref[b].astype(F32)
        )
        x, yl = b // 2, b % 2
        out_ref[((x * 2 + yh) * 2 + yl) * 2 + core, GROUP:] = total.astype(BF16)


def unpack_kernel(place_ref, in_ref, dq_ref, dk_ref, dv_ref):
    mine_yh, mine_core = place_ref[2], place_ref[0]
    for head in range(KEY_HEADS):
        x, yl = head // 2, head % 2
        parts = [
            in_ref[((x * 2 + yh) * 2 + yl) * 2 + core, :GROUP].astype(F32)
            for yh in range(2)
            for core in range(2)
        ]
        total = ((parts[0] + parts[1]) + (parts[2] + parts[3])).astype(BF16)
        for g in range(GROUP):
            n = head * GROUP + g
            dq_ref[:, n * HEAD_WIDTH : (n + 1) * HEAD_WIDTH] = total[g]
        cols = slice(head * HEAD_WIDTH, (head + 1) * HEAD_WIDTH)
        source = ((x * 2 + mine_yh) * 2 + yl) * 2 + mine_core
        dk_ref[:, cols] = in_ref[source, GROUP]
        dv_ref[:, cols] = in_ref[source, GROUP + 1]


def exchange(value, axes):
    return lax.all_to_all(value, axes, split_axis=0, concat_axis=0, tiled=True)


def along_z(value, steps):
    pairs = [(z, (z + steps) % 16) for z in range(16)]
    return lax.ppermute(value, ("zhi", "zlo"), pairs)


def active_lists(token_pos, block_mask):
    yh, zlo = lax.axis_index("yh"), lax.axis_index("zlo")
    block_ids = token_pos.reshape(64, BLK)[:, 0] // BLK
    by_place = block_ids.reshape(16, 4)
    query_pos = lax.dynamic_index_in_dim(by_place, zlo, 1, keepdims=False)
    mine = lax.dynamic_index_in_dim(block_ids.reshape(4, 2, 2, 4), yh, 1, keepdims=False)
    key_pos = jnp.concatenate(
        [
            lax.dynamic_index_in_dim(mine, (zlo + step) % 4, 2, keepdims=False).reshape(8)
            for step in STEPS
        ]
    )
    span = jnp.arange(64, dtype=jnp.int32)
    pick_query = (query_pos[:, None] == span[None, :]).astype(BF16)
    pick_key = (key_pos[:, None] == span[None, :]).astype(BF16)
    seen = jnp.dot(
        jnp.dot(pick_query, (block_mask == 1).astype(BF16), preferred_element_type=F32).astype(BF16),
        pick_key.T,
        preferred_element_type=F32,
    )
    active = (seen > 0.5) & (key_pos[None, :] <= query_pos[:, None])
    same = key_pos[None, :] == query_pos[:, None]
    number = jnp.arange(32, dtype=jnp.int32)
    ones = active.astype(jnp.int32)
    before = jnp.sum(
        jnp.where(number[None, None, :] < number[None, :, None], ones[:, None, :], 0), axis=2
    )
    count = jnp.sum(ones, axis=1)
    code = number[None, :] + 32 * same.astype(jnp.int32)
    lists = jnp.sum(
        jnp.where(active[:, None, :] & (before[:, None, :] == number[None, :, None]), code[:, None, :], 0),
        axis=2,
    )
    lists = jnp.where(number[None, :] < count[:, None], lists, 64)
    return jnp.concatenate([lists.reshape(512), jnp.full((32,), 64, jnp.int32)]), count


def local(
    queries,
    key_head_rows,
    value_head_rows,
    output_gradient,
    support_values,
    thresholds,
    gate_row_sums,
    token_pos,
    block_mask,
):
    shape = jax.ShapeDtypeStruct

    def by_head(stat):
        return stat.astype(F32).T.reshape(KEY_HEADS, GROUP * ROWS)

    place = jnp.stack([lax.axis_index(name) for name in ("core", "zhi", "yh")]).astype(jnp.int32)
    message = (ROWS, HEAD_WIDTH)
    send = vmem_call(pack_kernel, shape((16, SLOTS, *message), BF16), [WHOLE] * 7)(
        queries,
        output_gradient,
        support_values,
        by_head(thresholds),
        by_head(gate_row_sums),
        key_head_rows,
        value_head_rows,
    )
    arrived = exchange(send, PLANE)
    pieces = lax.dynamic_index_in_dim(
        arrived.reshape(4, 2, 2, SLOTS, *message)[:, :, :, 2 * GROUP + 1 :],
        lax.axis_index("yh"),
        1,
        keepdims=False,
    ).reshape(8, 2, *message)
    own = jnp.stack([pieces] + [along_z(pieces, -step * QUARTER) for step in STEPS[1:]], axis=1)
    near = [
        along_z(own, -1),
        along_z(own, 1),
        along_z(own[:4], -2),
        along_z(own[4:], 2),
    ]
    arrived_other = lax.ppermute(arrived, "core", [(0, 1), (1, 0)])
    lists, count = active_lists(token_pos, block_mask)

    def part(many):
        return shape((many, 4, 2, *message), BF16)

    piece = (PIECE, HEAD_WIDTH)
    grad_query, grad_own, *grad_near = vmem_call(
        attention_kernel,
        [shape((16, 2, GROUP * ROWS, HEAD_WIDTH), BF16)] + [part(m) for m in (8, 8, 8, 4, 4)],
        [SCALARS] * 3 + [WHOLE] * 7,
        scratch_shapes=[
            VMEM((32, *piece), BF16),
            VMEM((32, *piece), BF16),
            VMEM((3, PIECE, 256), F32),
            VMEM((32, *piece), F32),
            VMEM((32, *piece), F32),
            VMEM((16, HEAD_WIDTH, 256), F32),
            VMEM((16, 256, HEAD_WIDTH), BF16),
            VMEM((16, 256, HEAD_WIDTH), BF16),
            VMEM((16, 8, 256), F32),
            pltpu.SMEM((80,), jnp.int32),
        ],
    )(lists, count, place, arrived, arrived_other, own, *near)

    back = [
        along_z(grad, step) for grad, step in zip(grad_near, (1, -1, 2, -2), strict=True)
    ]
    eight = (8, 2, *message)
    first, *others = vmem_call(
        total_kernel, [shape(eight, F32)] + [shape(eight, BF16)] * 3, [WHOLE] * 5
    )(grad_own, *back)
    others = [along_z(grad, step * QUARTER) for grad, step in zip(others, STEPS[1:], strict=True)]
    send_back = vmem_call(
        merge_kernel, shape((32, GROUP + 2, *message), BF16), [SCALARS] + [WHOLE] * 5
    )(place, grad_query, first, *others)
    returned = exchange(send_back, PLANE + ("core",))
    return vmem_call(
        unpack_kernel,
        [
            shape((ROWS, QUERY_HEADS * HEAD_WIDTH), BF16),
            shape((ROWS, KEY_HEADS * HEAD_WIDTH), BF16),
            shape((ROWS, KEY_HEADS * HEAD_WIDTH), BF16),
        ],
        [SCALARS, WHOLE],
    )(place, returned)


def solution(mesh):
    parts = Mesh(
        mesh.devices.reshape(4, 2, 4, 2, 2, 4), ("zhi", "core", "x", "yh", "yl", "zlo")
    )
    rows = P(TOKEN_AXES, None)
    return jax.shard_map(
        local,
        mesh=parts,
        in_specs=(rows,) * 7 + (P(), P()),
        out_specs=(rows,) * 3,
        check_vma=False,
    )
```

```python
import functools

import jax
import jax.numpy as jnp
from jax import lax
from jax.experimental import pallas as pl
from jax.experimental.pallas import tpu as pltpu
from jax.sharding import Mesh, PartitionSpec as P

QUERY_HEADS = 64
KEY_HEADS = 8
HEAD_WIDTH = 128
BLK = 128
GROUP = 8
ROWS = 16
BATCH = 8
UNROLL = 3
SLOTS = 2 * GROUP + 1
PIECE = 64
SCALE = HEAD_WIDTH ** (-0.5)
FAR = 1e30
STEPS = (0, 1, -1, 2)
TOKEN_AXES = ("x", "yh", "yl", "zlo", "zhi", "core")
PLANE = ("x", "yh", "yl")
KEY_AXES = ("x", "yl", "zhi")
VMEM = pltpu.VMEM
F32 = jnp.float32
BF16 = jnp.bfloat16


def vmem_call(kernel, out_shape, ins, **kw):
    return pl.pallas_call(
        kernel,
        out_shape=out_shape,
        in_specs=ins,
        out_specs=jax.tree.map(lambda _: pl.BlockSpec(memory_space=VMEM), out_shape),
        compiler_params=pltpu.CompilerParams(vmem_limit_bytes=48 << 20),
        **kw,
    )


WHOLE = pl.BlockSpec(memory_space=VMEM)
SCALARS = pl.BlockSpec(memory_space=pltpu.SMEM)


def pack_keys_kernel(k_ref, v_ref, out_ref):
    for head in range(KEY_HEADS):
        cols = slice(head * HEAD_WIDTH, (head + 1) * HEAD_WIDTH)
        key, value = k_ref[:, cols], v_ref[:, cols]
        for copy in range(4):
            out_ref[head * 4 + copy, 0] = key
            out_ref[head * 4 + copy, 1] = value


def pack_queries_kernel(q_ref, do_ref, sup_ref, thr_ref, sums_ref, out_ref):
    for head in range(KEY_HEADS):
        dests = [(head // 2) * 4 + yh * 2 + head % 2 for yh in range(2)]
        products = []
        for g in range(GROUP):
            n = head * GROUP + g
            cols = slice(n * HEAD_WIDTH, (n + 1) * HEAD_WIDTH)
            query, grad = q_ref[:, cols], do_ref[:, cols]
            for dest in dests:
                out_ref[dest, g] = query
                out_ref[dest, GROUP + g] = grad
            products.append(grad.astype(F32) * sup_ref[:, cols].astype(F32))
        row_dot = jnp.sum(jnp.concatenate(products, axis=0).T, axis=0, keepdims=True)
        mean = row_dot / sums_ref[head : head + 1, :]
        high = mean.astype(BF16).astype(F32)
        low = mean - high
        stats = jnp.concatenate(
            [thr_ref[head : head + 1, :], high, low, jnp.zeros((13, 128), F32)], axis=0
        ).astype(BF16)
        for dest in dests:
            out_ref[dest, 2 * GROUP] = stats


def attention_kernel(
    list_ref,
    count_ref,
    place_ref,
    qa_ref,
    qb_ref,
    own_ref,
    up_ref,
    down_ref,
    far_a_ref,
    far_b_ref,
    dq_ref,
    own_out,
    up_out,
    down_out,
    far_a_out,
    far_b_out,
    k_s,
    v_s,
    bias_s,
    dk_s,
    dv_s,
    dqt_s,
    q_s,
    do_s,
    stat_s,
    work_s,
):
    core, zhi = place_ref[0], place_ref[1]
    ins = [own_ref, up_ref, down_ref, far_a_ref, far_b_ref]
    outs = [own_out, up_out, down_out, far_a_out, far_b_out]
    places = [(0, 8), (8, 8), (16, 8), (24, 4), (28, 4)]
    for ref, (first, many) in zip(ins, places):
        for b in range(many):
            k_s[first + b] = ref[b, :, 0].reshape(PIECE, HEAD_WIDTH)
            v_s[first + b] = ref[b, :, 1].reshape(PIECE, HEAD_WIDTH)
    dk_s[...] = jnp.zeros_like(dk_s)
    dv_s[...] = jnp.zeros_like(dv_s)
    dqt_s[...] = jnp.zeros_like(dqt_s)
    row = lax.broadcasted_iota(jnp.int32, (PIECE, 256), 0)
    lane = lax.broadcasted_iota(jnp.int32, (PIECE, 256), 1)
    key_offset = (row >> 4) * 32 + core * 16 + (row & 15)
    query_core = jnp.where(lane < 128, core, 1 - core)
    query_offset = zhi * 32 + query_core * 16 + (lane & 15)
    bias_s[0] = jnp.zeros((PIECE, 256), F32)
    bias_s[1] = jnp.where(key_offset <= query_offset, 0.0, FAR)
    bias_s[2] = jnp.full((PIECE, 256), FAR, F32)

    def prepare(j, total):
        pair = (qa_ref, qb_ref)
        tile = (GROUP * ROWS, HEAD_WIDTH)
        q_s[j] = jnp.concatenate([ref[j, :GROUP].reshape(tile) for ref in pair], axis=0)
        do_s[j] = jnp.concatenate(
            [ref[j, GROUP : 2 * GROUP].reshape(tile) for ref in pair], axis=0
        )
        stats = jnp.concatenate([ref[j, 2 * GROUP].astype(F32) for ref in pair], axis=1)
        stat_s[j, 0:1] = stats[0:1]
        stat_s[j, 1:2] = stats[1:2] + stats[2:3]

        def put(batch, at):
            work_s[at] = j * 32 + batch * BATCH
            return at + 1

        return lax.fori_loop(0, (count_ref[j] + BATCH - 1) // BATCH, put, total)

    total = lax.fori_loop(0, 16, prepare, jnp.int32(0))
    for extra in range(UNROLL - 1):
        work_s[total + extra] = 512

    def contract(a, b, a_dim, b_dim):
        return lax.dot_general(
            a, b, (((a_dim,), (b_dim,)), ((), ())), preferred_element_type=F32
        )

    def one_step(step, _):
        results = []
        for way in range(UNROLL):
            base = work_s[step * UNROLL + way]
            j = jnp.minimum(base >> 5, 15)
            entries = [list_ref[base + u] for u in range(BATCH)]
            ids = [entry & 31 for entry in entries]
            keys = jnp.concatenate([k_s[i] for i in ids], axis=0)
            values = jnp.concatenate([v_s[i] for i in ids], axis=0)
            bias = jnp.concatenate([bias_s[entry >> 5] for entry in entries], axis=0)
            query, grad = q_s[j], do_s[j]
            scores = contract(keys, query, 1, 1)
            dprob = contract(values, grad, 1, 1)
            gate = jnp.maximum(scores * (0.5 * SCALE) - stat_s[j, 0:1] - bias, 0.0)
            probs = (gate * gate).astype(BF16)
            dscore = (SCALE * gate * (dprob - stat_s[j, 1:2])).astype(BF16)
            dv = contract(probs, grad, 1, 0)
            dk = contract(dscore, query, 1, 0)
            results.append((j, ids, dk, dv, contract(keys, dscore, 0, 0)))
        for j, ids, dk, dv, dqt in results:
            dqt_s[j] += dqt
            for u, i in enumerate(ids):
                dk_s[i] += dk[u * PIECE : (u + 1) * PIECE]
                dv_s[i] += dv[u * PIECE : (u + 1) * PIECE]
        return 0

    lax.fori_loop(0, (total + UNROLL - 1) // UNROLL, one_step, 0)

    def finish(j, _):
        dq = dqt_s[j].T.astype(BF16)
        dq_ref[j, core] = dq[:128]
        dq_ref[j, 1 - core] = dq[128:]
        return 0

    lax.fori_loop(0, 16, finish, 0)
    for ref, (first, many) in zip(outs, places):
        for b in range(many):
            for kind, sums in enumerate((dk_s, dv_s)):
                ref[b, :, kind] = sums[first + b].astype(BF16).reshape(4, ROWS, HEAD_WIDTH)


def total_kernel(own_ref, up_ref, down_ref, far_a_ref, far_b_ref, out_ref):
    for b in range(8):
        far = far_a_ref[b] if b < 4 else far_b_ref[b - 4]
        total = (own_ref[b].astype(F32) + up_ref[b].astype(F32)) + (
            down_ref[b].astype(F32) + far.astype(F32)
        )
        out_ref[b] = total.astype(BF16)


def sum_queries_kernel(in_ref, out_ref):
    for head in range(KEY_HEADS):
        parts = [
            in_ref[(((head // 2) * 2 + yh) * 2 + head % 2) * 2 + core].astype(F32)
            for yh in range(2)
            for core in range(2)
        ]
        total = ((parts[0] + parts[1]) + (parts[2] + parts[3])).astype(BF16)
        for g in range(GROUP):
            n = head * GROUP + g
            out_ref[:, n * HEAD_WIDTH : (n + 1) * HEAD_WIDTH] = total[g * ROWS : (g + 1) * ROWS]


def sum_keys_kernel(in_ref, dk_ref, dv_ref):
    for head in range(KEY_HEADS):
        cols = slice(head * HEAD_WIDTH, (head + 1) * HEAD_WIDTH)
        for kind, ref in enumerate((dk_ref, dv_ref)):
            parts = [in_ref[head * 4 + zhi, kind].astype(F32) for zhi in range(4)]
            ref[:, cols] = ((parts[0] + parts[1]) + (parts[2] + parts[3])).astype(BF16)


def exchange(value, axes):
    return lax.all_to_all(value, axes, split_axis=0, concat_axis=0, tiled=True)


def along_z(value, steps):
    pairs = [(z, (z + steps) % 16) for z in range(16)]
    return lax.ppermute(value, ("zhi", "zlo"), pairs)


def active_lists(token_pos, block_mask):
    yh, zlo = lax.axis_index("yh"), lax.axis_index("zlo")
    block_ids = token_pos.reshape(64, BLK)[:, 0] // BLK
    by_place = block_ids.reshape(16, 4)
    query_pos = lax.dynamic_index_in_dim(by_place, zlo, 1, keepdims=False)
    mine = lax.dynamic_index_in_dim(block_ids.reshape(4, 2, 2, 4), yh, 1, keepdims=False)
    key_pos = jnp.concatenate(
        [
            lax.dynamic_index_in_dim(mine, (zlo + step) % 4, 2, keepdims=False).reshape(8)
            for step in STEPS
        ]
    )
    span = jnp.arange(64, dtype=jnp.int32)
    pick_query = (query_pos[:, None] == span[None, :]).astype(BF16)
    pick_key = (key_pos[:, None] == span[None, :]).astype(BF16)
    seen = jnp.dot(
        jnp.dot(pick_query, (block_mask == 1).astype(BF16), preferred_element_type=F32).astype(BF16),
        pick_key.T,
        preferred_element_type=F32,
    )
    active = (seen > 0.5) & (key_pos[None, :] <= query_pos[:, None])
    same = key_pos[None, :] == query_pos[:, None]
    number = jnp.arange(32, dtype=jnp.int32)
    ones = active.astype(jnp.int32)
    before = jnp.sum(
        jnp.where(number[None, None, :] < number[None, :, None], ones[:, None, :], 0), axis=2
    )
    count = jnp.sum(ones, axis=1)
    code = number[None, :] + 32 * same.astype(jnp.int32)
    lists = jnp.sum(
        jnp.where(active[:, None, :] & (before[:, None, :] == number[None, :, None]), code[:, None, :], 0),
        axis=2,
    )
    lists = jnp.where(number[None, :] < count[:, None], lists, 64)
    return jnp.concatenate([lists.reshape(512), jnp.full((32,), 64, jnp.int32)]), count


def local(
    queries,
    key_head_rows,
    value_head_rows,
    output_gradient,
    support_values,
    thresholds,
    gate_row_sums,
    token_pos,
    block_mask,
):
    shape = jax.ShapeDtypeStruct

    def by_head(stat):
        return stat.astype(F32).T.reshape(KEY_HEADS, GROUP * ROWS)

    place = jnp.stack([lax.axis_index(name) for name in ("core", "zhi")]).astype(jnp.int32)
    message = (ROWS, HEAD_WIDTH)
    send_keys = vmem_call(pack_keys_kernel, shape((32, 2, *message), BF16), [WHOLE] * 2)(
        key_head_rows, value_head_rows
    )
    own = exchange(send_keys, KEY_AXES).reshape(8, 4, 2, *message)
    send = vmem_call(pack_queries_kernel, shape((16, SLOTS, *message), BF16), [WHOLE] * 5)(
        queries,
        output_gradient,
        support_values,
        by_head(thresholds),
        by_head(gate_row_sums),
    )
    send, own = lax.optimization_barrier((send, own))
    near = [
        along_z(own, -1),
        along_z(own, 1),
        along_z(own[:4], -2),
        along_z(own[4:], 2),
    ]
    arrived = exchange(send, PLANE)
    arrived, *near = lax.optimization_barrier((arrived, *near))
    arrived_other = lax.ppermute(arrived, "core", [(0, 1), (1, 0)])
    lists, count = active_lists(token_pos, block_mask)

    def part(many):
        return shape((many, 4, 2, *message), BF16)

    piece = (PIECE, HEAD_WIDTH)
    grad_query, grad_own, *grad_near = vmem_call(
        attention_kernel,
        [shape((16, 2, GROUP * ROWS, HEAD_WIDTH), BF16)] + [part(m) for m in (8, 8, 8, 4, 4)],
        [SCALARS] * 3 + [WHOLE] * 7,
        scratch_shapes=[
            VMEM((32, *piece), BF16),
            VMEM((32, *piece), BF16),
            VMEM((3, PIECE, 256), F32),
            VMEM((32, *piece), F32),
            VMEM((32, *piece), F32),
            VMEM((16, HEAD_WIDTH, 256), F32),
            VMEM((16, 256, HEAD_WIDTH), BF16),
            VMEM((16, 256, HEAD_WIDTH), BF16),
            VMEM((16, 8, 256), F32),
            pltpu.SMEM((80,), jnp.int32),
        ],
    )(lists, count, place, arrived, arrived_other, own, *near)

    back = [
        along_z(grad, step) for grad, step in zip(grad_near, (1, -1, 2, -2), strict=True)
    ]
    back_query = exchange(
        grad_query.reshape(32, GROUP * ROWS, HEAD_WIDTH), PLANE + ("core",)
    )
    query_out = vmem_call(
        sum_queries_kernel, shape((ROWS, QUERY_HEADS * HEAD_WIDTH), BF16), [WHOLE]
    )(back_query)
    total = vmem_call(total_kernel, part(8), [WHOLE] * 5)(grad_own, *back)
    back_keys = exchange(total.reshape(32, 2, *message), KEY_AXES)
    key_shape = shape((ROWS, KEY_HEADS * HEAD_WIDTH), BF16)
    key_out, value_out = vmem_call(sum_keys_kernel, [key_shape, key_shape], [WHOLE])(back_keys)
    return query_out, key_out, value_out


def solution(mesh):
    parts = Mesh(
        mesh.devices.reshape(4, 2, 4, 2, 2, 4), ("zhi", "core", "x", "yh", "yl", "zlo")
    )
    rows = P(TOKEN_AXES, None)
    return jax.shard_map(
        local,
        mesh=parts,
        in_specs=(rows,) * 7 + (P(), P()),
        out_specs=(rows,) * 3,
        check_vma=False,
    )
```

```python
import functools

import jax
import jax.numpy as jnp
from jax import lax
from jax.experimental import pallas as pl
from jax.experimental.pallas import tpu as pltpu
from jax.sharding import Mesh, PartitionSpec as P

QUERY_HEADS = 64
KEY_HEADS = 8
HEAD_WIDTH = 128
BLK = 128
GROUP = 8
ROWS = 16
OWN, REST = 8, 24
BATCH = {OWN: 4, REST: 8}
UNROLL = {OWN: 4, REST: 3}
SLOTS = 2 * GROUP + 1
PIECE = 64
SCALE = HEAD_WIDTH ** (-0.5)
FAR = 1e30
STEPS = (0, 1, -1, 2)
QUARTER = 4
TOKEN_AXES = ("x", "yh", "yl", "zlo", "zhi", "core")
PLANE = ("x", "yh", "yl")
HEAD_AXES = ("x", "yl")
KEY_AXES = ("x", "yl", "zhi")
VMEM = pltpu.VMEM
F32 = jnp.float32
BF16 = jnp.bfloat16


def vmem_call(kernel, out_shape, ins, **kw):
    return pl.pallas_call(
        kernel,
        out_shape=out_shape,
        in_specs=ins,
        out_specs=jax.tree.map(lambda _: pl.BlockSpec(memory_space=VMEM), out_shape),
        compiler_params=pltpu.CompilerParams(vmem_limit_bytes=20 << 20),
        **kw,
    )


WHOLE = pl.BlockSpec(memory_space=VMEM)
SCALARS = pl.BlockSpec(memory_space=pltpu.SMEM)


def pack_keys_kernel(k_ref, v_ref, out_ref):
    for head in range(KEY_HEADS):
        cols = slice(head * HEAD_WIDTH, (head + 1) * HEAD_WIDTH)
        out_ref[head, 0] = k_ref[:, cols]
        out_ref[head, 1] = v_ref[:, cols]


def pack_queries_kernel(q_ref, do_ref, sup_ref, thr_ref, sums_ref, out_ref):
    for head in range(KEY_HEADS):
        dests = [(head // 2) * 4 + yh * 2 + head % 2 for yh in range(2)]
        products = []
        for g in range(GROUP):
            n = head * GROUP + g
            cols = slice(n * HEAD_WIDTH, (n + 1) * HEAD_WIDTH)
            query, grad = q_ref[:, cols], do_ref[:, cols]
            for dest in dests:
                out_ref[dest, g] = query
                out_ref[dest, GROUP + g] = grad
            products.append(grad.astype(F32) * sup_ref[:, cols].astype(F32))
        row_dot = jnp.sum(jnp.concatenate(products, axis=0).T, axis=0, keepdims=True)
        mean = row_dot / sums_ref[head : head + 1, :]
        high = mean.astype(BF16).astype(F32)
        low = mean - high
        stats = jnp.concatenate(
            [thr_ref[head : head + 1, :], high, low, jnp.zeros((13, 128), F32)], axis=0
        ).astype(BF16)
        for dest in dests:
            out_ref[dest, 2 * GROUP] = stats


def contract(a, b, a_dim, b_dim):
    return lax.dot_general(a, b, (((a_dim,), (b_dim,)), ((), ())), preferred_element_type=F32)


def load_keys(refs, k_s, v_s):
    at = 0
    for ref in refs:
        for b in range(ref.shape[0]):
            k_s[at] = ref[b, :, 0].reshape(PIECE, HEAD_WIDTH)
            v_s[at] = ref[b, :, 1].reshape(PIECE, HEAD_WIDTH)
            at += 1


def store_keys(refs, dk_s, dv_s):
    at = 0
    for ref in refs:
        for b in range(ref.shape[0]):
            for kind, sums in enumerate((dk_s, dv_s)):
                ref[b, :, kind] = sums[at].astype(BF16).reshape(4, ROWS, HEAD_WIDTH)
            at += 1


def add_tiles(
    pieces, list_ref, count_ref, k_s, v_s, dk_s, dv_s, dqt_s, q_s, do_s, stat_s, work_s, bias_s
):
    batch, unroll = BATCH[pieces], UNROLL[pieces]

    def plan(j, total):
        def put(step, at):
            work_s[at] = j * pieces + step * batch
            return at + 1

        return lax.fori_loop(0, (count_ref[j] + batch - 1) // batch, put, total)

    total = lax.fori_loop(0, 16, plan, jnp.int32(0))
    for extra in range(unroll - 1):
        work_s[total + extra] = 16 * pieces

    def one_step(step, _):
        results = []
        for way in range(unroll):
            base = work_s[step * unroll + way]
            j = jnp.minimum(base // pieces, 15)
            entries = [list_ref[base + u] for u in range(batch)]
            ids = [entry & 31 for entry in entries]
            keys = jnp.concatenate([k_s[i] for i in ids], axis=0)
            values = jnp.concatenate([v_s[i] for i in ids], axis=0)
            query, grad = q_s[j], do_s[j]
            thresh = stat_s[j, 0:1]
            scores = contract(keys, query, 1, 1) * (0.5 * SCALE)
            if bias_s is None:
                above = jnp.concatenate(
                    [
                        scores[u * PIECE : (u + 1) * PIECE]
                        - (thresh + jnp.where(entry >= 64, FAR, 0.0))
                        for u, entry in enumerate(entries)
                    ],
                    axis=0,
                )
            else:
                bias = jnp.concatenate([bias_s[entry >> 5] for entry in entries], axis=0)
                above = scores - thresh - bias
            gate = jnp.maximum(above, 0.0)
            dprob = contract(values, grad, 1, 1)
            probs = (gate * gate).astype(BF16)
            dscore = (SCALE * gate * (dprob - stat_s[j, 1:2])).astype(BF16)
            dv = contract(probs, grad, 1, 0)
            dk = contract(dscore, query, 1, 0)
            results.append((j, ids, dk, dv, contract(keys, dscore, 0, 0)))
        for j, ids, dk, dv, dqt in results:
            dqt_s[j] += dqt
            for u, i in enumerate(ids):
                dk_s[i] += dk[u * PIECE : (u + 1) * PIECE]
                dv_s[i] += dv[u * PIECE : (u + 1) * PIECE]
        return 0

    lax.fori_loop(0, (total + unroll - 1) // unroll, one_step, 0)


def own_kernel(
    list_ref,
    count_ref,
    place_ref,
    qa_ref,
    qb_ref,
    own_ref,
    own_out,
    dqt_s,
    q_s,
    do_s,
    stat_s,
    k_s,
    v_s,
    bias_s,
    dk_s,
    dv_s,
    work_s,
):
    core, zhi = place_ref[0], place_ref[1]
    load_keys([own_ref], k_s, v_s)
    dk_s[...] = jnp.zeros_like(dk_s)
    dv_s[...] = jnp.zeros_like(dv_s)
    dqt_s[...] = jnp.zeros_like(dqt_s)
    row = lax.broadcasted_iota(jnp.int32, (PIECE, 256), 0)
    lane = lax.broadcasted_iota(jnp.int32, (PIECE, 256), 1)
    part = row >> 4
    step = jnp.where(part == 0, 0, jnp.where(part == 1, 1, jnp.where(part == 2, 3, 2)))
    key_offset = ((zhi + step) & 3) * 32 + core * 16 + (row & 15)
    query_core = jnp.where(lane < 128, core, 1 - core)
    query_offset = zhi * 32 + query_core * 16 + (lane & 15)
    bias_s[0] = jnp.zeros((PIECE, 256), F32)
    bias_s[1] = jnp.where(key_offset <= query_offset, 0.0, FAR)
    bias_s[2] = jnp.full((PIECE, 256), FAR, F32)

    def prepare(j, _):
        pair = (qa_ref, qb_ref)
        tile = (GROUP * ROWS, HEAD_WIDTH)
        q_s[j] = jnp.concatenate([ref[j, :GROUP].reshape(tile) for ref in pair], axis=0)
        do_s[j] = jnp.concatenate(
            [ref[j, GROUP : 2 * GROUP].reshape(tile) for ref in pair], axis=0
        )
        stats = jnp.concatenate([ref[j, 2 * GROUP].astype(F32) for ref in pair], axis=1)
        stat_s[j, 0:1] = stats[0:1]
        stat_s[j, 1:2] = stats[1:2] + stats[2:3]
        return 0

    lax.fori_loop(0, 16, prepare, 0)
    add_tiles(
        OWN, list_ref, count_ref, k_s, v_s, dk_s, dv_s, dqt_s, q_s, do_s, stat_s, work_s, bias_s
    )
    store_keys([own_out], dk_s, dv_s)


def rest_kernel(
    list_ref,
    count_ref,
    place_ref,
    dqt_in,
    q_s,
    do_s,
    stat_s,
    up_ref,
    down_ref,
    far_a_ref,
    far_b_ref,
    dq_ref,
    up_out,
    down_out,
    far_a_out,
    far_b_out,
    k_s,
    v_s,
    dk_s,
    dv_s,
    dqt_s,
    work_s,
):
    core = place_ref[0]
    load_keys([up_ref, down_ref, far_a_ref, far_b_ref], k_s, v_s)
    dk_s[...] = jnp.zeros_like(dk_s)
    dv_s[...] = jnp.zeros_like(dv_s)
    dqt_s[...] = dqt_in[...]
    add_tiles(
        REST, list_ref, count_ref, k_s, v_s, dk_s, dv_s, dqt_s, q_s, do_s, stat_s, work_s, None
    )

    def finish(j, _):
        dq = dqt_s[j].T.astype(BF16)
        dq_ref[j, core] = dq[:128]
        dq_ref[j, 1 - core] = dq[128:]
        return 0

    lax.fori_loop(0, 16, finish, 0)
    store_keys([up_out, down_out, far_a_out, far_b_out], dk_s, dv_s)


def total_kernel(place_ref, own_ref, up_ref, down_ref, far_a_ref, far_b_ref, out_ref):
    for b in range(8):
        far = far_a_ref[b] if b < 4 else far_b_ref[b - 4]
        total = (own_ref[b].astype(F32) + up_ref[b].astype(F32)) + (
            down_ref[b].astype(F32) + far.astype(F32)
        )
        for part, step in enumerate(STEPS):
            out_ref[b, (place_ref[1] + step) & 3] = total[part].astype(BF16)


def sum_queries_kernel(in_ref, out_ref):
    for head in range(KEY_HEADS):
        parts = [
            in_ref[(((head // 2) * 2 + yh) * 2 + head % 2) * 2 + core].astype(F32)
            for yh in range(2)
            for core in range(2)
        ]
        total = ((parts[0] + parts[1]) + (parts[2] + parts[3])).astype(BF16)
        for g in range(GROUP):
            n = head * GROUP + g
            out_ref[:, n * HEAD_WIDTH : (n + 1) * HEAD_WIDTH] = total[g * ROWS : (g + 1) * ROWS]


def sum_keys_kernel(in_ref, dk_ref, dv_ref):
    for head in range(KEY_HEADS):
        cols = slice(head * HEAD_WIDTH, (head + 1) * HEAD_WIDTH)
        for kind, ref in enumerate((dk_ref, dv_ref)):
            parts = [in_ref[head * 4 + zhi, kind].astype(F32) for zhi in range(4)]
            ref[:, cols] = ((parts[0] + parts[1]) + (parts[2] + parts[3])).astype(BF16)


def exchange(value, axes):
    return lax.all_to_all(value, axes, split_axis=0, concat_axis=0, tiled=True)


def along_z(value, steps):
    pairs = [(z, (z + steps) % 16) for z in range(16)]
    return lax.ppermute(value, ("zhi", "zlo"), pairs)


def active_lists(token_pos, block_mask):
    yh, zlo = lax.axis_index("yh"), lax.axis_index("zlo")
    block_ids = token_pos.reshape(64, BLK)[:, 0] // BLK
    by_place = block_ids.reshape(16, 4)
    query_pos = lax.dynamic_index_in_dim(by_place, zlo, 1, keepdims=False)
    mine = lax.dynamic_index_in_dim(block_ids.reshape(4, 2, 2, 4), yh, 1, keepdims=False)
    key_pos = jnp.concatenate(
        [
            lax.dynamic_index_in_dim(mine, (zlo + step) % 4, 2, keepdims=False).reshape(8)
            for step in STEPS
        ]
    )
    span = jnp.arange(64, dtype=jnp.int32)
    pick_query = (query_pos[:, None] == span[None, :]).astype(BF16)
    pick_key = (key_pos[:, None] == span[None, :]).astype(BF16)
    seen = jnp.dot(
        jnp.dot(pick_query, (block_mask == 1).astype(BF16), preferred_element_type=F32).astype(BF16),
        pick_key.T,
        preferred_element_type=F32,
    )
    active = (seen > 0.5) & (key_pos[None, :] <= query_pos[:, None])
    same = key_pos[None, :] == query_pos[:, None]

    def packed(first, many):
        seen = active[:, first : first + many]
        number = jnp.arange(many, dtype=jnp.int32)
        ones = seen.astype(jnp.int32)
        before = jnp.sum(
            jnp.where(number[None, None, :] < number[None, :, None], ones[:, None, :], 0), axis=2
        )
        count = jnp.sum(ones, axis=1)
        code = number[None, :] + 32 * same[:, first : first + many].astype(jnp.int32)
        place = seen[:, None, :] & (before[:, None, :] == number[None, :, None])
        lists = jnp.sum(jnp.where(place, code[:, None, :], 0), axis=2)
        lists = jnp.where(number[None, :] < count[:, None], lists, 64)
        lists = jnp.concatenate([lists.reshape(16 * many), jnp.full((32,), 64, jnp.int32)])
        return lists, count

    return packed(0, OWN), packed(OWN, REST)


def local(
    queries,
    key_head_rows,
    value_head_rows,
    output_gradient,
    support_values,
    thresholds,
    gate_row_sums,
    token_pos,
    block_mask,
):
    shape = jax.ShapeDtypeStruct

    def by_head(stat):
        return stat.astype(F32).T.reshape(KEY_HEADS, GROUP * ROWS)

    place = jnp.stack([lax.axis_index(name) for name in ("core", "zhi")]).astype(jnp.int32)
    message = (ROWS, HEAD_WIDTH)
    send_keys = vmem_call(pack_keys_kernel, shape((KEY_HEADS, 2, *message), BF16), [WHOLE] * 2)(
        key_head_rows, value_head_rows
    )
    pieces = exchange(send_keys, HEAD_AXES)
    send = vmem_call(pack_queries_kernel, shape((16, SLOTS, *message), BF16), [WHOLE] * 5)(
        queries,
        output_gradient,
        support_values,
        by_head(thresholds),
        by_head(gate_row_sums),
    )
    send, pieces = lax.optimization_barrier((send, pieces))
    others = [along_z(pieces, -step * QUARTER) for step in STEPS[1:]]
    arrived = exchange(send, PLANE)
    arrived, *others = lax.optimization_barrier((arrived, *others))
    own = jnp.stack([pieces, *others], axis=1)
    near = [
        along_z(own, -1),
        along_z(own, 1),
        along_z(own[:4], -2),
        along_z(own[4:], 2),
    ]
    arrived_other = lax.ppermute(arrived, "core", [(0, 1), (1, 0)])
    own_lists, rest_lists = active_lists(token_pos, block_mask)

    def part(many):
        return shape((many, 4, 2, *message), BF16)

    piece = (PIECE, HEAD_WIDTH)
    query_shape = (16, 256, HEAD_WIDTH)
    dqt_shape = (16, HEAD_WIDTH, 256)

    def key_scratch(many):
        return [VMEM((many, *piece), BF16)] * 2, [VMEM((many, *piece), F32)] * 2

    inputs, sums = key_scratch(OWN)
    grad_own, *state = vmem_call(
        own_kernel,
        [
            part(8),
            shape(dqt_shape, F32),
            shape(query_shape, BF16),
            shape(query_shape, BF16),
            shape((16, 8, 256), F32),
        ],
        [SCALARS] * 3 + [WHOLE] * 3,
        scratch_shapes=[
            *inputs,
            VMEM((3, PIECE, 256), F32),
            *sums,
            pltpu.SMEM((64,), jnp.int32),
        ],
        cost_estimate=pl.CostEstimate(
            flops=4_000_000_000, bytes_accessed=8 << 20, transcendentals=0
        ),
    )(*own_lists, place, arrived, arrived_other, own)
    inputs, sums = key_scratch(REST)
    grad_query, *grad_near = vmem_call(
        rest_kernel,
        [shape((16, 2, GROUP * ROWS, HEAD_WIDTH), BF16)] + [part(m) for m in (8, 8, 4, 4)],
        [SCALARS] * 3 + [WHOLE] * 8,
        scratch_shapes=[
            *inputs,
            *sums,
            VMEM(dqt_shape, F32),
            pltpu.SMEM((64,), jnp.int32),
        ],
    )(*rest_lists, place, *state, *near)

    back = [
        along_z(grad, step) for grad, step in zip(grad_near, (1, -1, 2, -2), strict=True)
    ]
    back_query = exchange(
        grad_query.reshape(32, GROUP * ROWS, HEAD_WIDTH), PLANE + ("core",)
    )
    query_out = vmem_call(
        sum_queries_kernel, shape((ROWS, QUERY_HEADS * HEAD_WIDTH), BF16), [WHOLE]
    )(back_query)
    total = vmem_call(total_kernel, part(8), [SCALARS] + [WHOLE] * 5)(place, grad_own, *back)
    back_keys = exchange(total.reshape(32, 2, *message), KEY_AXES)
    key_shape = shape((ROWS, KEY_HEADS * HEAD_WIDTH), BF16)
    key_out, value_out = vmem_call(sum_keys_kernel, [key_shape, key_shape], [WHOLE])(back_keys)
    return query_out, key_out, value_out


def solution(mesh):
    parts = Mesh(
        mesh.devices.reshape(4, 2, 4, 2, 2, 4), ("zhi", "core", "x", "yh", "yl", "zlo")
    )
    rows = P(TOKEN_AXES, None)
    return jax.shard_map(
        local,
        mesh=parts,
        in_specs=(rows,) * 7 + (P(), P()),
        out_specs=(rows,) * 3,
        check_vma=False,
    )
```

```python
import functools

import jax
import jax.numpy as jnp
from jax import lax
from jax.experimental import pallas as pl
from jax.experimental.pallas import tpu as pltpu
from jax.sharding import Mesh, PartitionSpec as P

QUERY_HEADS = 64
KEY_HEADS = 8
HEAD_WIDTH = 128
BLK = 128
GROUP = 8
ROWS = 16
BATCH = 8
UNROLL = 3
SLOTS = 2 * GROUP + 1
PIECE = 64
SCALE = HEAD_WIDTH ** (-0.5)
FAR = 1e30
STEPS = (0, 1, -1, 2)
TOKEN_AXES = ("x", "yh", "yl", "zlo", "zhi", "core")
PLANE = ("x", "yh", "yl")
KEY_AXES = ("x", "yl", "zhi")
VMEM = pltpu.VMEM
F32 = jnp.float32
BF16 = jnp.bfloat16


def vmem_call(kernel, out_shape, ins, mib=20, **kw):
    return pl.pallas_call(
        kernel,
        out_shape=out_shape,
        in_specs=ins,
        out_specs=jax.tree.map(lambda _: pl.BlockSpec(memory_space=VMEM), out_shape),
        compiler_params=pltpu.CompilerParams(vmem_limit_bytes=mib << 20),
        **kw,
    )


WHOLE = pl.BlockSpec(memory_space=VMEM)
SCALARS = pl.BlockSpec(memory_space=pltpu.SMEM)


def pack_keys_kernel(k_ref, v_ref, out_ref):
    for head in range(KEY_HEADS):
        cols = slice(head * HEAD_WIDTH, (head + 1) * HEAD_WIDTH)
        key, value = k_ref[:, cols], v_ref[:, cols]
        for copy in range(4):
            out_ref[head * 4 + copy, 0] = key
            out_ref[head * 4 + copy, 1] = value


def pack_queries_kernel(q_ref, do_ref, sup_ref, thr_ref, sums_ref, out_ref):
    for head in range(KEY_HEADS):
        dests = [(head // 2) * 4 + yh * 2 + head % 2 for yh in range(2)]
        products = []
        for g in range(GROUP):
            n = head * GROUP + g
            cols = slice(n * HEAD_WIDTH, (n + 1) * HEAD_WIDTH)
            query, grad = q_ref[:, cols], do_ref[:, cols]
            for dest in dests:
                out_ref[dest, g] = query
                out_ref[dest, GROUP + g] = grad
            products.append(grad.astype(F32) * sup_ref[:, cols].astype(F32))
        row_dot = jnp.sum(jnp.concatenate(products, axis=0).T, axis=0, keepdims=True)
        mean = row_dot / sums_ref[head : head + 1, :]
        high = mean.astype(BF16).astype(F32)
        low = mean - high
        stats = jnp.concatenate(
            [thr_ref[head : head + 1, :], high, low, jnp.zeros((13, 128), F32)], axis=0
        ).astype(BF16)
        for dest in dests:
            out_ref[dest, 2 * GROUP] = stats


def attention_kernel(
    list_ref,
    count_ref,
    place_ref,
    qa_ref,
    qb_ref,
    own_ref,
    up_ref,
    down_ref,
    far_a_ref,
    far_b_ref,
    dq_ref,
    own_out,
    up_out,
    down_out,
    far_a_out,
    far_b_out,
    k_s,
    v_s,
    bias_s,
    dk_s,
    dv_s,
    dqt_s,
    stat_s,
    work_s,
):
    core, zhi = place_ref[0], place_ref[1]
    ins = [own_ref, up_ref, down_ref, far_a_ref, far_b_ref]
    outs = [own_out, up_out, down_out, far_a_out, far_b_out]
    places = [(0, 8), (8, 8), (16, 8), (24, 4), (28, 4)]
    for ref, (first, many) in zip(ins, places):
        for b in range(many):
            k_s[first + b] = ref[b, :, 0].reshape(PIECE, HEAD_WIDTH)
            v_s[first + b] = ref[b, :, 1].reshape(PIECE, HEAD_WIDTH)
    dk_s[...] = jnp.zeros_like(dk_s)
    dv_s[...] = jnp.zeros_like(dv_s)
    dqt_s[...] = jnp.zeros_like(dqt_s)
    row = lax.broadcasted_iota(jnp.int32, (PIECE, 256), 0)
    lane = lax.broadcasted_iota(jnp.int32, (PIECE, 256), 1)
    key_offset = (row >> 4) * 32 + core * 16 + (row & 15)
    query_core = jnp.where(lane < 128, core, 1 - core)
    query_offset = zhi * 32 + query_core * 16 + (lane & 15)
    bias_s[0] = jnp.zeros((PIECE, 256), F32)
    bias_s[1] = jnp.where(key_offset <= query_offset, 0.0, FAR)
    bias_s[2] = jnp.full((PIECE, 256), FAR, F32)

    def prepare(j, total):
        stats = jnp.concatenate(
            [ref[j, 2 * GROUP].astype(F32) for ref in (qa_ref, qb_ref)], axis=1
        )
        stat_s[j, 0:1] = stats[0:1]
        stat_s[j, 1:2] = stats[1:2] + stats[2:3]

        def put(batch, at):
            work_s[at] = j * 32 + batch * BATCH
            return at + 1

        return lax.fori_loop(0, (count_ref[j] + BATCH - 1) // BATCH, put, total)

    total = lax.fori_loop(0, 16, prepare, jnp.int32(0))
    for extra in range(UNROLL - 1):
        work_s[total + extra] = 512

    def contract(a, b, a_dim, b_dim):
        return lax.dot_general(
            a, b, (((a_dim,), (b_dim,)), ((), ())), preferred_element_type=F32
        )

    def rows(j, first):
        return jnp.concatenate(
            [
                ref[j, first : first + GROUP].reshape(GROUP * ROWS, HEAD_WIDTH)
                for ref in (qa_ref, qb_ref)
            ],
            axis=0,
        )

    def one_step(step, _):
        results = []
        for way in range(UNROLL):
            base = work_s[step * UNROLL + way]
            j = jnp.minimum(base >> 5, 15)
            entries = [list_ref[base + u] for u in range(BATCH)]
            ids = [entry & 31 for entry in entries]
            keys = jnp.concatenate([k_s[i] for i in ids], axis=0)
            values = jnp.concatenate([v_s[i] for i in ids], axis=0)
            bias = jnp.concatenate([bias_s[entry >> 5] for entry in entries], axis=0)
            query, grad = rows(j, 0), rows(j, GROUP)
            scores = contract(keys, query, 1, 1)
            dprob = contract(values, grad, 1, 1)
            gate = jnp.maximum(scores * (0.5 * SCALE) - stat_s[j, 0:1] - bias, 0.0)
            probs = (gate * gate).astype(BF16)
            dscore = (SCALE * gate * (dprob - stat_s[j, 1:2])).astype(BF16)
            dv = contract(probs, grad, 1, 0)
            dk = contract(dscore, query, 1, 0)
            results.append((j, ids, dk, dv, contract(keys, dscore, 0, 0)))
        for j, ids, dk, dv, dqt in results:
            dqt_s[j] += dqt
            for u, i in enumerate(ids):
                dk_s[i] += dk[u * PIECE : (u + 1) * PIECE]
                dv_s[i] += dv[u * PIECE : (u + 1) * PIECE]
        return 0

    lax.fori_loop(0, (total + UNROLL - 1) // UNROLL, one_step, 0)

    def finish(j, _):
        dq = dqt_s[j].T.astype(BF16)
        dq_ref[j, core] = dq[:128]
        dq_ref[j, 1 - core] = dq[128:]
        return 0

    lax.fori_loop(0, 16, finish, 0)
    for ref, (first, many) in zip(outs, places):
        for b in range(many):
            for kind, sums in enumerate((dk_s, dv_s)):
                ref[b, :, kind] = sums[first + b].astype(BF16).reshape(4, ROWS, HEAD_WIDTH)


def total_kernel(own_ref, up_ref, down_ref, far_a_ref, far_b_ref, out_ref):
    for b in range(8):
        far = far_a_ref[b] if b < 4 else far_b_ref[b - 4]
        total = (own_ref[b].astype(F32) + up_ref[b].astype(F32)) + (
            down_ref[b].astype(F32) + far.astype(F32)
        )
        out_ref[b] = total.astype(BF16)


def sum_queries_kernel(in_ref, out_ref):
    for head in range(KEY_HEADS):
        parts = [
            in_ref[(((head // 2) * 2 + yh) * 2 + head % 2) * 2 + core].astype(F32)
            for yh in range(2)
            for core in range(2)
        ]
        total = ((parts[0] + parts[1]) + (parts[2] + parts[3])).astype(BF16)
        for g in range(GROUP):
            n = head * GROUP + g
            out_ref[:, n * HEAD_WIDTH : (n + 1) * HEAD_WIDTH] = total[g * ROWS : (g + 1) * ROWS]


def sum_keys_kernel(in_ref, dk_ref, dv_ref):
    for head in range(KEY_HEADS):
        cols = slice(head * HEAD_WIDTH, (head + 1) * HEAD_WIDTH)
        for kind, ref in enumerate((dk_ref, dv_ref)):
            parts = [in_ref[head * 4 + zhi, kind].astype(F32) for zhi in range(4)]
            ref[:, cols] = ((parts[0] + parts[1]) + (parts[2] + parts[3])).astype(BF16)


def exchange(value, axes):
    return lax.all_to_all(value, axes, split_axis=0, concat_axis=0, tiled=True)


def along_z(value, steps):
    pairs = [(z, (z + steps) % 16) for z in range(16)]
    return lax.ppermute(value, ("zhi", "zlo"), pairs)


def active_lists(token_pos, block_mask):
    yh, zlo = lax.axis_index("yh"), lax.axis_index("zlo")
    block_ids = token_pos.reshape(64, BLK)[:, 0] // BLK
    by_place = block_ids.reshape(16, 4)
    query_pos = lax.dynamic_index_in_dim(by_place, zlo, 1, keepdims=False)
    mine = lax.dynamic_index_in_dim(block_ids.reshape(4, 2, 2, 4), yh, 1, keepdims=False)
    key_pos = jnp.concatenate(
        [
            lax.dynamic_index_in_dim(mine, (zlo + step) % 4, 2, keepdims=False).reshape(8)
            for step in STEPS
        ]
    )
    span = jnp.arange(64, dtype=jnp.int32)
    pick_query = (query_pos[:, None] == span[None, :]).astype(BF16)
    pick_key = (key_pos[:, None] == span[None, :]).astype(BF16)
    seen = jnp.dot(
        jnp.dot(pick_query, (block_mask == 1).astype(BF16), preferred_element_type=F32).astype(BF16),
        pick_key.T,
        preferred_element_type=F32,
    )
    active = (seen > 0.5) & (key_pos[None, :] <= query_pos[:, None])
    same = key_pos[None, :] == query_pos[:, None]
    number = jnp.arange(32, dtype=jnp.int32)
    ones = active.astype(jnp.int32)
    before = jnp.sum(
        jnp.where(number[None, None, :] < number[None, :, None], ones[:, None, :], 0), axis=2
    )
    count = jnp.sum(ones, axis=1)
    code = number[None, :] + 32 * same.astype(jnp.int32)
    lists = jnp.sum(
        jnp.where(active[:, None, :] & (before[:, None, :] == number[None, :, None]), code[:, None, :], 0),
        axis=2,
    )
    lists = jnp.where(number[None, :] < count[:, None], lists, 64)
    return jnp.concatenate([lists.reshape(512), jnp.full((32,), 64, jnp.int32)]), count


def local(
    queries,
    key_head_rows,
    value_head_rows,
    output_gradient,
    support_values,
    thresholds,
    gate_row_sums,
    token_pos,
    block_mask,
):
    shape = jax.ShapeDtypeStruct

    def by_head(stat):
        return stat.astype(F32).T.reshape(KEY_HEADS, GROUP * ROWS)

    place = jnp.stack([lax.axis_index(name) for name in ("core", "zhi")]).astype(jnp.int32)
    message = (ROWS, HEAD_WIDTH)
    send_keys = vmem_call(pack_keys_kernel, shape((32, 2, *message), BF16), [WHOLE] * 2, 60)(
        key_head_rows, value_head_rows
    )
    own = exchange(send_keys, KEY_AXES).reshape(8, 4, 2, *message)
    send = vmem_call(pack_queries_kernel, shape((16, SLOTS, *message), BF16), [WHOLE] * 5)(
        queries,
        output_gradient,
        support_values,
        by_head(thresholds),
        by_head(gate_row_sums),
    )
    send, own = lax.optimization_barrier((send, own))
    near = [
        along_z(own, -1),
        along_z(own, 1),
        along_z(own[:4], -2),
        along_z(own[4:], 2),
    ]
    arrived = exchange(send, PLANE)
    arrived, *near = lax.optimization_barrier((arrived, *near))
    arrived_other = lax.ppermute(arrived, "core", [(0, 1), (1, 0)])
    lists, count = active_lists(token_pos, block_mask)

    def part(many):
        return shape((many, 4, 2, *message), BF16)

    piece = (PIECE, HEAD_WIDTH)
    grad_query, grad_own, *grad_near = vmem_call(
        attention_kernel,
        [shape((16, 2, GROUP * ROWS, HEAD_WIDTH), BF16)] + [part(m) for m in (8, 8, 8, 4, 4)],
        [SCALARS] * 3 + [WHOLE] * 7,
        60,
        scratch_shapes=[
            VMEM((32, *piece), BF16),
            VMEM((32, *piece), BF16),
            VMEM((3, PIECE, 256), F32),
            VMEM((32, *piece), F32),
            VMEM((32, *piece), F32),
            VMEM((16, HEAD_WIDTH, 256), F32),
            VMEM((16, 8, 256), F32),
            pltpu.SMEM((80,), jnp.int32),
        ],
    )(lists, count, place, arrived, arrived_other, own, *near)

    back = [
        along_z(grad, step) for grad, step in zip(grad_near, (1, -1, 2, -2), strict=True)
    ]
    back_query = exchange(
        grad_query.reshape(32, GROUP * ROWS, HEAD_WIDTH), PLANE + ("core",)
    )
    query_out = vmem_call(
        sum_queries_kernel, shape((ROWS, QUERY_HEADS * HEAD_WIDTH), BF16), [WHOLE]
    )(back_query)
    total = vmem_call(total_kernel, part(8), [WHOLE] * 5)(grad_own, *back)
    back_keys = exchange(total.reshape(32, 2, *message), KEY_AXES)
    key_shape = shape((ROWS, KEY_HEADS * HEAD_WIDTH), BF16)
    key_out, value_out = vmem_call(sum_keys_kernel, [key_shape, key_shape], [WHOLE])(back_keys)
    return query_out, key_out, value_out


def solution(mesh):
    parts = Mesh(
        mesh.devices.reshape(4, 2, 4, 2, 2, 4), ("zhi", "core", "x", "yh", "yl", "zlo")
    )
    rows = P(TOKEN_AXES, None)
    return jax.shard_map(
        local,
        mesh=parts,
        in_specs=(rows,) * 7 + (P(), P()),
        out_specs=(rows,) * 3,
        check_vma=False,
    )
```

```python
import functools

import jax
import jax.numpy as jnp
from jax import lax
from jax.experimental import pallas as pl
from jax.experimental.pallas import tpu as pltpu
from jax.sharding import Mesh, PartitionSpec as P

QUERY_HEADS = 64
KEY_HEADS = 8
HEAD_WIDTH = 128
BLK = 128
GROUP = 8
ROWS = 16
BATCH = 8
UNROLL = 3
SLOTS = 2 * GROUP + 1
PIECE = 64
SCALE = HEAD_WIDTH ** (-0.5)
FAR = 1e30
STEPS = (0, 1, -1, 2)
TOKEN_AXES = ("x", "yh", "yl", "zlo", "zhi", "core")
PLANE = ("x", "yh", "yl")
HEAD_AXES = ("x", "yl")
KEY_AXES = ("zhi", "x", "yl")
VMEM = pltpu.VMEM
F32 = jnp.float32
BF16 = jnp.bfloat16


def vmem_call(kernel, out_shape, ins, mib=20, **kw):
    return pl.pallas_call(
        kernel,
        out_shape=out_shape,
        in_specs=ins,
        out_specs=jax.tree.map(lambda _: pl.BlockSpec(memory_space=VMEM), out_shape),
        compiler_params=pltpu.CompilerParams(vmem_limit_bytes=mib << 20),
        **kw,
    )


WHOLE = pl.BlockSpec(memory_space=VMEM)
SCALARS = pl.BlockSpec(memory_space=pltpu.SMEM)


def pack_keys_kernel(k_ref, v_ref, out_ref):
    for head in range(KEY_HEADS):
        cols = slice(head * HEAD_WIDTH, (head + 1) * HEAD_WIDTH)
        out_ref[head, 0] = k_ref[:, cols]
        out_ref[head, 1] = v_ref[:, cols]


def pack_queries_kernel(q_ref, do_ref, sup_ref, thr_ref, sums_ref, out_ref):
    wide = (QUERY_HEADS, GROUP * ROWS)
    column = lax.broadcasted_iota(jnp.int32, wide, 0)
    lane_head = lax.broadcasted_iota(jnp.int32, wide, 1) >> 4
    tall = (ROWS, GROUP * ROWS)
    own_row = lax.broadcasted_iota(jnp.int32, tall, 0) == (
        lax.broadcasted_iota(jnp.int32, tall, 1) & (ROWS - 1)
    )

    def to_lanes(ref, head):
        pick = (column == head * GROUP + lane_head).astype(BF16)
        spread = jnp.dot(ref[...], pick, preferred_element_type=F32)
        return jnp.sum(jnp.where(own_row, spread, 0.0), axis=0, keepdims=True)

    for head in range(KEY_HEADS):
        dests = [(head // 2) * 4 + yh * 2 + head % 2 for yh in range(2)]
        products = []
        for g in range(GROUP):
            n = head * GROUP + g
            cols = slice(n * HEAD_WIDTH, (n + 1) * HEAD_WIDTH)
            query, grad = q_ref[:, cols], do_ref[:, cols]
            for dest in dests:
                out_ref[dest, g] = query
                out_ref[dest, GROUP + g] = grad
            products.append(grad.astype(F32) * sup_ref[:, cols].astype(F32))
        row_dot = jnp.sum(jnp.concatenate(products, axis=0).T, axis=0, keepdims=True)
        mean = row_dot / to_lanes(sums_ref, head)
        high = mean.astype(BF16).astype(F32)
        low = mean - high
        stats = jnp.concatenate(
            [to_lanes(thr_ref, head), high, low, jnp.zeros((13, 128), F32)], axis=0
        ).astype(BF16)
        for dest in dests:
            out_ref[dest, 2 * GROUP] = stats


def attention_kernel(
    list_ref,
    count_ref,
    place_ref,
    qa_ref,
    qb_ref,
    own_ref,
    up_ref,
    down_ref,
    far_a_ref,
    far_b_ref,
    dq_ref,
    own_out,
    up_out,
    down_out,
    far_a_out,
    far_b_out,
    k_s,
    v_s,
    bias_s,
    dk_s,
    dv_s,
    dqt_s,
    stat_s,
    work_s,
):
    core, zhi = place_ref[0], place_ref[1]
    ins = [own_ref, up_ref, down_ref, far_a_ref, far_b_ref]
    outs = [own_out, up_out, down_out, far_a_out, far_b_out]
    places = [(0, 8), (8, 8), (16, 8), (24, 4), (28, 4)]
    for ref, (first, many) in zip(ins, places):
        for b in range(many):
            k_s[first + b] = ref[b, :, 0].reshape(PIECE, HEAD_WIDTH)
            v_s[first + b] = ref[b, :, 1].reshape(PIECE, HEAD_WIDTH)
    dk_s[...] = jnp.zeros_like(dk_s)
    dv_s[...] = jnp.zeros_like(dv_s)
    dqt_s[...] = jnp.zeros_like(dqt_s)
    row = lax.broadcasted_iota(jnp.int32, (PIECE, 256), 0)
    lane = lax.broadcasted_iota(jnp.int32, (PIECE, 256), 1)
    key_offset = (row >> 4) * 32 + core * 16 + (row & 15)
    query_core = jnp.where(lane < 128, core, 1 - core)
    query_offset = zhi * 32 + query_core * 16 + (lane & 15)
    bias_s[0] = jnp.zeros((PIECE, 256), F32)
    bias_s[1] = jnp.where(key_offset <= query_offset, 0.0, FAR)
    bias_s[2] = jnp.full((PIECE, 256), FAR, F32)

    def prepare(j, total):
        stats = jnp.concatenate(
            [ref[j, 2 * GROUP].astype(F32) for ref in (qa_ref, qb_ref)], axis=1
        )
        stat_s[j, 0:1] = stats[0:1]
        stat_s[j, 1:2] = stats[1:2] + stats[2:3]

        def put(batch, at):
            work_s[at] = j * 32 + batch * BATCH
            return at + 1

        return lax.fori_loop(0, (count_ref[j] + BATCH - 1) // BATCH, put, total)

    total = lax.fori_loop(0, 16, prepare, jnp.int32(0))
    for extra in range(UNROLL - 1):
        work_s[total + extra] = 512

    def contract(a, b, a_dim, b_dim):
        return lax.dot_general(
            a, b, (((a_dim,), (b_dim,)), ((), ())), preferred_element_type=F32
        )

    def rows(j, first):
        return jnp.concatenate(
            [
                ref[j, first : first + GROUP].reshape(GROUP * ROWS, HEAD_WIDTH)
                for ref in (qa_ref, qb_ref)
            ],
            axis=0,
        )

    def one_step(step, _):
        results = []
        for way in range(UNROLL):
            base = work_s[step * UNROLL + way]
            j = jnp.minimum(base >> 5, 15)
            entries = [list_ref[base + u] for u in range(BATCH)]
            ids = [entry & 31 for entry in entries]
            keys = jnp.concatenate([k_s[i] for i in ids], axis=0)
            values = jnp.concatenate([v_s[i] for i in ids], axis=0)
            bias = jnp.concatenate([bias_s[entry >> 5] for entry in entries], axis=0)
            query, grad = rows(j, 0), rows(j, GROUP)
            scores = contract(keys, query, 1, 1)
            dprob = contract(values, grad, 1, 1)
            gate = jnp.maximum(scores * (0.5 * SCALE) - stat_s[j, 0:1] - bias, 0.0)
            probs = (gate * gate).astype(BF16)
            dscore = (SCALE * gate * (dprob - stat_s[j, 1:2])).astype(BF16)
            dv = contract(probs, grad, 1, 0)
            dk = contract(dscore, query, 1, 0)
            results.append((j, ids, dk, dv, contract(keys, dscore, 0, 0)))
        for j, ids, dk, dv, dqt in results:
            dqt_s[j] += dqt
            for u, i in enumerate(ids):
                dk_s[i] += dk[u * PIECE : (u + 1) * PIECE]
                dv_s[i] += dv[u * PIECE : (u + 1) * PIECE]
        return 0

    lax.fori_loop(0, (total + UNROLL - 1) // UNROLL, one_step, 0)

    def finish(j, _):
        dq = dqt_s[j].T.astype(BF16)
        dq_ref[j, core] = dq[:128]
        dq_ref[j, 1 - core] = dq[128:]
        return 0

    lax.fori_loop(0, 16, finish, 0)
    for ref, (first, many) in zip(outs, places):
        for b in range(many):
            for kind, sums in enumerate((dk_s, dv_s)):
                ref[b, :, kind] = sums[first + b].astype(BF16).reshape(4, ROWS, HEAD_WIDTH)


def total_kernel(own_ref, up_ref, down_ref, far_a_ref, far_b_ref, out_ref):
    for b in range(8):
        far = far_a_ref[b] if b < 4 else far_b_ref[b - 4]
        total = (own_ref[b].astype(F32) + up_ref[b].astype(F32)) + (
            down_ref[b].astype(F32) + far.astype(F32)
        )
        out_ref[:, b] = total.astype(BF16)


def sum_queries_kernel(in_ref, out_ref):
    for head in range(KEY_HEADS):
        parts = [
            in_ref[(((head // 2) * 2 + yh) * 2 + head % 2) * 2 + core].astype(F32)
            for yh in range(2)
            for core in range(2)
        ]
        total = ((parts[0] + parts[1]) + (parts[2] + parts[3])).astype(BF16)
        for g in range(GROUP):
            n = head * GROUP + g
            out_ref[:, n * HEAD_WIDTH : (n + 1) * HEAD_WIDTH] = total[g * ROWS : (g + 1) * ROWS]


def sum_keys_kernel(in_ref, dk_ref, dv_ref):
    for head in range(KEY_HEADS):
        cols = slice(head * HEAD_WIDTH, (head + 1) * HEAD_WIDTH)
        for kind, ref in enumerate((dk_ref, dv_ref)):
            parts = [in_ref[zhi * 8 + head, kind].astype(F32) for zhi in range(4)]
            ref[:, cols] = ((parts[0] + parts[1]) + (parts[2] + parts[3])).astype(BF16)


def exchange(value, axes):
    return lax.all_to_all(value, axes, split_axis=0, concat_axis=0, tiled=True)


def along_z(value, steps):
    pairs = [(z, (z + steps) % 16) for z in range(16)]
    return lax.ppermute(value, ("zhi", "zlo"), pairs)


def active_lists(token_pos, block_mask):
    yh, zlo = lax.axis_index("yh"), lax.axis_index("zlo")
    block_ids = token_pos.reshape(64, BLK)[:, 0] // BLK
    by_place = block_ids.reshape(16, 4)
    query_pos = lax.dynamic_index_in_dim(by_place, zlo, 1, keepdims=False)
    mine = lax.dynamic_index_in_dim(block_ids.reshape(4, 2, 2, 4), yh, 1, keepdims=False)
    key_pos = jnp.concatenate(
        [
            lax.dynamic_index_in_dim(mine, (zlo + step) % 4, 2, keepdims=False).reshape(8)
            for step in STEPS
        ]
    )
    span = jnp.arange(64, dtype=jnp.int32)
    pick_query = (query_pos[:, None] == span[None, :]).astype(BF16)
    pick_key = (key_pos[:, None] == span[None, :]).astype(BF16)
    seen = jnp.dot(
        jnp.dot(pick_query, (block_mask == 1).astype(BF16), preferred_element_type=F32).astype(BF16),
        pick_key.T,
        preferred_element_type=F32,
    )
    active = (seen > 0.5) & (key_pos[None, :] <= query_pos[:, None])
    same = key_pos[None, :] == query_pos[:, None]
    number = jnp.arange(32, dtype=jnp.int32)
    ones = active.astype(jnp.int32)
    before = jnp.sum(
        jnp.where(number[None, None, :] < number[None, :, None], ones[:, None, :], 0), axis=2
    )
    count = jnp.sum(ones, axis=1)
    code = number[None, :] + 32 * same.astype(jnp.int32)
    lists = jnp.sum(
        jnp.where(active[:, None, :] & (before[:, None, :] == number[None, :, None]), code[:, None, :], 0),
        axis=2,
    )
    lists = jnp.where(number[None, :] < count[:, None], lists, 64)
    return jnp.concatenate([lists.reshape(512), jnp.full((32,), 64, jnp.int32)]), count


def local(
    queries,
    key_head_rows,
    value_head_rows,
    output_gradient,
    support_values,
    thresholds,
    gate_row_sums,
    token_pos,
    block_mask,
):
    shape = jax.ShapeDtypeStruct

    place = jnp.stack([lax.axis_index(name) for name in ("core", "zhi")]).astype(jnp.int32)
    message = (ROWS, HEAD_WIDTH)
    send_keys = vmem_call(pack_keys_kernel, shape((8, 2, *message), BF16), [WHOLE] * 2, 60)(
        key_head_rows, value_head_rows
    )
    own = jnp.swapaxes(lax.all_gather(exchange(send_keys, HEAD_AXES), "zhi", axis=0), 0, 1)
    send = vmem_call(pack_queries_kernel, shape((16, SLOTS, *message), BF16), [WHOLE] * 5, 60)(
        queries,
        output_gradient,
        support_values,
        thresholds,
        gate_row_sums,
    )
    send, own = lax.optimization_barrier((send, own))
    near = [
        along_z(own, -1),
        along_z(own, 1),
        along_z(own[:4], -2),
        along_z(own[4:], 2),
    ]
    arrived = exchange(send, PLANE)
    arrived, *near = lax.optimization_barrier((arrived, *near))
    arrived_other = lax.ppermute(arrived, "core", [(0, 1), (1, 0)])
    token_pos, _ = lax.optimization_barrier((token_pos, own[0, 0, 0, 0, 0]))
    lists, count = active_lists(token_pos, block_mask)

    def part(many):
        return shape((many, 4, 2, *message), BF16)

    piece = (PIECE, HEAD_WIDTH)
    grad_query, grad_own, *grad_near = vmem_call(
        attention_kernel,
        [shape((16, 2, GROUP * ROWS, HEAD_WIDTH), BF16)] + [part(m) for m in (8, 8, 8, 4, 4)],
        [SCALARS] * 3 + [WHOLE] * 7,
        60,
        scratch_shapes=[
            VMEM((32, *piece), BF16),
            VMEM((32, *piece), BF16),
            VMEM((3, PIECE, 256), F32),
            VMEM((32, *piece), F32),
            VMEM((32, *piece), F32),
            VMEM((16, HEAD_WIDTH, 256), F32),
            VMEM((16, 8, 256), F32),
            pltpu.SMEM((80,), jnp.int32),
        ],
    )(lists, count, place, arrived, arrived_other, own, *near)

    back = [
        along_z(grad, step) for grad, step in zip(grad_near, (1, -1, 2, -2), strict=True)
    ]
    back_query = exchange(
        grad_query.reshape(32, GROUP * ROWS, HEAD_WIDTH), PLANE + ("core",)
    )
    query_out = vmem_call(
        sum_queries_kernel, shape((ROWS, QUERY_HEADS * HEAD_WIDTH), BF16), [WHOLE]
    )(back_query)
    total = vmem_call(total_kernel, shape((4, 8, 2, *message), BF16), [WHOLE] * 5)(
        grad_own, *back
    )
    back_keys = exchange(total.reshape(32, 2, *message), KEY_AXES)
    key_shape = shape((ROWS, KEY_HEADS * HEAD_WIDTH), BF16)
    key_out, value_out = vmem_call(sum_keys_kernel, [key_shape, key_shape], [WHOLE])(back_keys)
    return query_out, key_out, value_out


def solution(mesh):
    parts = Mesh(
        mesh.devices.reshape(4, 2, 4, 2, 2, 4), ("zhi", "core", "x", "yh", "yl", "zlo")
    )
    rows = P(TOKEN_AXES, None)
    return jax.shard_map(
        local,
        mesh=parts,
        in_specs=(rows,) * 7 + (P(), P()),
        out_specs=(rows,) * 3,
        check_vma=False,
    )
```

```python
import functools

import jax
import jax.numpy as jnp
from jax import lax
from jax.experimental import pallas as pl
from jax.experimental.pallas import tpu as pltpu
from jax.sharding import Mesh, PartitionSpec as P

QUERY_HEADS = 64
KEY_HEADS = 8
HEAD_WIDTH = 128
BLK = 128
GROUP = 8
ROWS = 16
BATCH = 8
UNROLL = 3
SLOTS = 2 * GROUP + 1
PIECE = 64
SCALE = HEAD_WIDTH ** (-0.5)
FAR = 1e30
STEPS = (0, 1, -1, 2)
TOKEN_AXES = ("x", "yh", "yl", "zlo", "zhi", "core")
PLANE = ("x", "yh", "yl")
HEAD_AXES = ("x", "yl")
KEY_AXES = ("zhi", "x", "yl")
VMEM = pltpu.VMEM
F32 = jnp.float32
BF16 = jnp.bfloat16


def vmem_call(kernel, out_shape, ins, mib=20, **kw):
    return pl.pallas_call(
        kernel,
        out_shape=out_shape,
        in_specs=ins,
        out_specs=jax.tree.map(lambda _: pl.BlockSpec(memory_space=VMEM), out_shape),
        compiler_params=pltpu.CompilerParams(vmem_limit_bytes=mib << 20),
        **kw,
    )


WHOLE = pl.BlockSpec(memory_space=VMEM)
SCALARS = pl.BlockSpec(memory_space=pltpu.SMEM)


def pack_keys_kernel(k_ref, v_ref, out_ref):
    for head in range(KEY_HEADS):
        cols = slice(head * HEAD_WIDTH, (head + 1) * HEAD_WIDTH)
        out_ref[head, 0] = k_ref[:, cols]
        out_ref[head, 1] = v_ref[:, cols]


def pack_queries_kernel(q_ref, do_ref, sup_ref, thr_ref, sums_ref, out_ref):
    wide = (QUERY_HEADS, GROUP * ROWS)
    column = lax.broadcasted_iota(jnp.int32, wide, 0)
    lane_head = lax.broadcasted_iota(jnp.int32, wide, 1) >> 4
    tall = (ROWS, GROUP * ROWS)
    own_row = lax.broadcasted_iota(jnp.int32, tall, 0) == (
        lax.broadcasted_iota(jnp.int32, tall, 1) & (ROWS - 1)
    )

    def to_lanes(ref, head):
        pick = (column == head * GROUP + lane_head).astype(BF16)
        spread = jnp.dot(ref[...], pick, preferred_element_type=F32)
        return jnp.sum(jnp.where(own_row, spread, 0.0), axis=0, keepdims=True)

    for head in range(KEY_HEADS):
        dests = [(head // 2) * 4 + yh * 2 + head % 2 for yh in range(2)]
        products = []
        for g in range(GROUP):
            n = head * GROUP + g
            cols = slice(n * HEAD_WIDTH, (n + 1) * HEAD_WIDTH)
            query, grad = q_ref[:, cols], do_ref[:, cols]
            for dest in dests:
                out_ref[dest, g] = query
                out_ref[dest, GROUP + g] = grad
            products.append(grad.astype(F32) * sup_ref[:, cols].astype(F32))
        row_dot = jnp.sum(jnp.concatenate(products, axis=0).T, axis=0, keepdims=True)
        mean = row_dot / to_lanes(sums_ref, head)
        high = mean.astype(BF16).astype(F32)
        low = mean - high
        stats = jnp.concatenate(
            [to_lanes(thr_ref, head), high, low, jnp.zeros((13, 128), F32)], axis=0
        ).astype(BF16)
        for dest in dests:
            out_ref[dest, 2 * GROUP] = stats


def attention_kernel(
    list_ref,
    count_ref,
    qa_ref,
    qb_ref,
    own_ref,
    up_ref,
    down_ref,
    far_a_ref,
    far_b_ref,
    dq_ref,
    own_out,
    up_out,
    down_out,
    far_a_out,
    far_b_out,
    k_s,
    v_s,
    bias_s,
    dk_s,
    dv_s,
    dqt_s,
    stat_s,
    work_s,
):
    core, zhi = lax.axis_index("core"), lax.axis_index("zhi")
    ins = [own_ref, up_ref, down_ref, far_a_ref, far_b_ref]
    outs = [own_out, up_out, down_out, far_a_out, far_b_out]
    places = [(0, 8), (8, 8), (16, 8), (24, 4), (28, 4)]
    for ref, (first, many) in zip(ins, places):
        for b in range(many):
            k_s[first + b] = ref[b, :, 0].reshape(PIECE, HEAD_WIDTH)
            v_s[first + b] = ref[b, :, 1].reshape(PIECE, HEAD_WIDTH)
    dk_s[...] = jnp.zeros_like(dk_s)
    dv_s[...] = jnp.zeros_like(dv_s)
    dqt_s[...] = jnp.zeros_like(dqt_s)
    row = lax.broadcasted_iota(jnp.int32, (PIECE, 256), 0)
    lane = lax.broadcasted_iota(jnp.int32, (PIECE, 256), 1)
    key_offset = (row >> 4) * 32 + core * 16 + (row & 15)
    query_core = jnp.where(lane < 128, core, 1 - core)
    query_offset = zhi * 32 + query_core * 16 + (lane & 15)
    bias_s[0] = jnp.zeros((PIECE, 256), F32)
    bias_s[1] = jnp.where(key_offset <= query_offset, 0.0, FAR)
    bias_s[2] = jnp.full((PIECE, 256), FAR, F32)

    def prepare(j, total):
        stats = jnp.concatenate(
            [ref[j, 2 * GROUP].astype(F32) for ref in (qa_ref, qb_ref)], axis=1
        )
        stat_s[j, 0:1] = stats[0:1]
        stat_s[j, 1:2] = stats[1:2] + stats[2:3]

        def put(batch, at):
            work_s[at] = j * 32 + batch * BATCH
            return at + 1

        return lax.fori_loop(0, (count_ref[j] + BATCH - 1) // BATCH, put, total)

    total = lax.fori_loop(0, 16, prepare, jnp.int32(0))
    for extra in range(UNROLL - 1):
        work_s[total + extra] = 512

    def contract(a, b, a_dim, b_dim):
        return lax.dot_general(
            a, b, (((a_dim,), (b_dim,)), ((), ())), preferred_element_type=F32
        )

    def rows(j, first):
        return jnp.concatenate(
            [
                ref[j, first : first + GROUP].reshape(GROUP * ROWS, HEAD_WIDTH)
                for ref in (qa_ref, qb_ref)
            ],
            axis=0,
        )

    def one_step(step, _):
        results = []
        for way in range(UNROLL):
            base = work_s[step * UNROLL + way]
            j = jnp.minimum(base >> 5, 15)
            entries = [
                jnp.where(base >= 512, 64, list_ref[j, (base & 31) + u]) for u in range(BATCH)
            ]
            ids = [entry & 31 for entry in entries]
            keys = jnp.concatenate([k_s[i] for i in ids], axis=0)
            values = jnp.concatenate([v_s[i] for i in ids], axis=0)
            bias = jnp.concatenate([bias_s[entry >> 5] for entry in entries], axis=0)
            query, grad = rows(j, 0), rows(j, GROUP)
            scores = contract(keys, query, 1, 1)
            dprob = contract(values, grad, 1, 1)
            gate = jnp.maximum(scores * (0.5 * SCALE) - stat_s[j, 0:1] - bias, 0.0)
            probs = (gate * gate).astype(BF16)
            dscore = (SCALE * gate * (dprob - stat_s[j, 1:2])).astype(BF16)
            dv = contract(probs, grad, 1, 0)
            dk = contract(dscore, query, 1, 0)
            results.append((j, ids, dk, dv, contract(keys, dscore, 0, 0)))
        for j, ids, dk, dv, dqt in results:
            dqt_s[j] += dqt
            for u, i in enumerate(ids):
                dk_s[i] += dk[u * PIECE : (u + 1) * PIECE]
                dv_s[i] += dv[u * PIECE : (u + 1) * PIECE]
        return 0

    lax.fori_loop(0, (total + UNROLL - 1) // UNROLL, one_step, 0)

    def finish(j, _):
        dq = dqt_s[j].T.astype(BF16)
        dq_ref[j, core] = dq[:128]
        dq_ref[j, 1 - core] = dq[128:]
        return 0

    lax.fori_loop(0, 16, finish, 0)
    for ref, (first, many) in zip(outs, places):
        for b in range(many):
            for kind, sums in enumerate((dk_s, dv_s)):
                ref[b, :, kind] = sums[first + b].astype(BF16).reshape(4, ROWS, HEAD_WIDTH)


def total_kernel(own_ref, up_ref, down_ref, far_a_ref, far_b_ref, out_ref):
    for b in range(8):
        far = far_a_ref[b] if b < 4 else far_b_ref[b - 4]
        total = (own_ref[b].astype(F32) + up_ref[b].astype(F32)) + (
            down_ref[b].astype(F32) + far.astype(F32)
        )
        out_ref[:, b] = total.astype(BF16)


def sum_queries_kernel(in_ref, out_ref):
    for head in range(KEY_HEADS):
        parts = [
            in_ref[(((head // 2) * 2 + yh) * 2 + head % 2) * 2 + core].astype(F32)
            for yh in range(2)
            for core in range(2)
        ]
        total = ((parts[0] + parts[1]) + (parts[2] + parts[3])).astype(BF16)
        for g in range(GROUP):
            n = head * GROUP + g
            out_ref[:, n * HEAD_WIDTH : (n + 1) * HEAD_WIDTH] = total[g * ROWS : (g + 1) * ROWS]


def sum_keys_kernel(in_ref, dk_ref, dv_ref):
    for head in range(KEY_HEADS):
        cols = slice(head * HEAD_WIDTH, (head + 1) * HEAD_WIDTH)
        for kind, ref in enumerate((dk_ref, dv_ref)):
            parts = [in_ref[zhi * 8 + head, kind].astype(F32) for zhi in range(4)]
            ref[:, cols] = ((parts[0] + parts[1]) + (parts[2] + parts[3])).astype(BF16)


def exchange(value, axes):
    return lax.all_to_all(value, axes, split_axis=0, concat_axis=0, tiled=True)


def along_z(value, steps):
    pairs = [(z, (z + steps) % 16) for z in range(16)]
    return lax.ppermute(value, ("zhi", "zlo"), pairs)


def active_lists(token_pos, block_mask):
    yh, zlo = lax.axis_index("yh"), lax.axis_index("zlo")
    block_ids = token_pos.reshape(64, BLK)[:, 0] // BLK
    by_place = block_ids.reshape(16, 4)
    query_pos = lax.dynamic_index_in_dim(by_place, zlo, 1, keepdims=False)
    mine = lax.dynamic_index_in_dim(block_ids.reshape(4, 2, 2, 4), yh, 1, keepdims=False)
    key_pos = jnp.concatenate(
        [
            lax.dynamic_index_in_dim(mine, (zlo + step) % 4, 2, keepdims=False).reshape(8)
            for step in STEPS
        ]
    )
    span = jnp.arange(64, dtype=jnp.int32)
    pick_query = (query_pos[:, None] == span[None, :]).astype(BF16)
    pick_key = (key_pos[:, None] == span[None, :]).astype(BF16)
    seen = jnp.dot(
        jnp.dot(pick_query, (block_mask == 1).astype(BF16), preferred_element_type=F32).astype(BF16),
        pick_key.T,
        preferred_element_type=F32,
    )
    active = (seen > 0.5) & (key_pos[None, :] <= query_pos[:, None])
    same = key_pos[None, :] == query_pos[:, None]
    number = jnp.arange(32, dtype=jnp.int32)
    ones = active.astype(jnp.int32)
    before = jnp.sum(
        jnp.where(number[None, None, :] < number[None, :, None], ones[:, None, :], 0), axis=2
    )
    count = jnp.sum(ones, axis=1)
    code = number[None, :] + 32 * same.astype(jnp.int32)
    lists = jnp.sum(
        jnp.where(active[:, None, :] & (before[:, None, :] == number[None, :, None]), code[:, None, :], 0),
        axis=2,
    )
    lists = jnp.where(number[None, :] < count[:, None], lists, 64)
    return lists, count


def local(
    queries,
    key_head_rows,
    value_head_rows,
    output_gradient,
    support_values,
    thresholds,
    gate_row_sums,
    token_pos,
    block_mask,
):
    shape = jax.ShapeDtypeStruct

    message = (ROWS, HEAD_WIDTH)
    send_keys = vmem_call(pack_keys_kernel, shape((8, 2, *message), BF16), [WHOLE] * 2, 60)(
        key_head_rows, value_head_rows
    )
    own = jnp.swapaxes(lax.all_gather(exchange(send_keys, HEAD_AXES), "zhi", axis=0), 0, 1)
    send = vmem_call(pack_queries_kernel, shape((16, SLOTS, *message), BF16), [WHOLE] * 5, 60)(
        queries,
        output_gradient,
        support_values,
        thresholds,
        gate_row_sums,
    )
    send, own = lax.optimization_barrier((send, own))
    near = [
        along_z(own, -1),
        along_z(own, 1),
        along_z(own[:4], -2),
        along_z(own[4:], 2),
    ]
    arrived = exchange(send, PLANE)
    arrived, *near = lax.optimization_barrier((arrived, *near))
    arrived_other = lax.ppermute(arrived, "core", [(0, 1), (1, 0)])
    token_pos, _ = lax.optimization_barrier((token_pos, own[0, 0, 0, 0, 0]))
    lists, count = active_lists(token_pos, block_mask)

    def part(many):
        return shape((many, 4, 2, *message), BF16)

    piece = (PIECE, HEAD_WIDTH)
    grad_query, grad_own, *grad_near = vmem_call(
        attention_kernel,
        [shape((16, 2, GROUP * ROWS, HEAD_WIDTH), BF16)] + [part(m) for m in (8, 8, 8, 4, 4)],
        [SCALARS] * 2 + [WHOLE] * 7,
        60,
        scratch_shapes=[
            VMEM((32, *piece), BF16),
            VMEM((32, *piece), BF16),
            VMEM((3, PIECE, 256), F32),
            VMEM((32, *piece), F32),
            VMEM((32, *piece), F32),
            VMEM((16, HEAD_WIDTH, 256), F32),
            VMEM((16, 8, 256), F32),
            pltpu.SMEM((80,), jnp.int32),
        ],
    )(lists, count, arrived, arrived_other, own, *near)

    back = [
        along_z(grad, step) for grad, step in zip(grad_near, (1, -1, 2, -2), strict=True)
    ]
    back_query = exchange(
        grad_query.reshape(32, GROUP * ROWS, HEAD_WIDTH), PLANE + ("core",)
    )
    query_out = vmem_call(
        sum_queries_kernel, shape((ROWS, QUERY_HEADS * HEAD_WIDTH), BF16), [WHOLE]
    )(back_query)
    total = vmem_call(total_kernel, shape((4, 8, 2, *message), BF16), [WHOLE] * 5)(
        grad_own, *back
    )
    back_keys = exchange(total.reshape(32, 2, *message), KEY_AXES)
    key_shape = shape((ROWS, KEY_HEADS * HEAD_WIDTH), BF16)
    key_out, value_out = vmem_call(sum_keys_kernel, [key_shape, key_shape], [WHOLE])(back_keys)
    return query_out, key_out, value_out


def solution(mesh):
    parts = Mesh(
        mesh.devices.reshape(4, 2, 4, 2, 2, 4), ("zhi", "core", "x", "yh", "yl", "zlo")
    )
    rows = P(TOKEN_AXES, None)
    return jax.shard_map(
        local,
        mesh=parts,
        in_specs=(rows,) * 7 + (P(), P()),
        out_specs=(rows,) * 3,
        check_vma=False,
    )
```
